32 devices in a mesh: row: 4 (over y, core), col: 8 (over z, x).
Axes of the slice: x: 2, y: 2, z: 4, core: 2. Of those that a mesh axis runs over, the one named last changes fastest.
Arguments:
- tensor: float32 [32, 1024, 2048], P(None, 'row', 'col'), may hold values from -120 to 120
- factor_b: float32 [2048, 256], P('col', 'row'), may hold values from -1 to 1
- factor_c: float32 [32, 256], replicated, may hold values from -5 to 5
Outputs:
- factor_a: float32 [1024, 256], P(('row', 'col'))
- col_scale: float32 [256], replicated
The draws below stay inside these ranges and needn't reach their ends.
All inputs are finite; a program needn't handle non-finite values.
Results may differ from the reference program's by a relative error of at most 0.0003.
Values sent between devices are 32-bit elements; how exact they have to be, the bound alone decides.
A program may use at most 64 MiB of HBM per device.

```python
import jax
import jax.numpy as jnp
from jax import lax

K = 32
R = 256
I = 1024
J = 2048


def draw_tensor(key, part):
    key = jax.random.fold_in(key, 11)
    first, second = jax.random.split(key, 2)
    rise = 3.0 ** (jnp.arange(I, dtype=jnp.float32) / I)
    spread = jnp.exp(jax.random.uniform(second, (I,), minval=0.0, maxval=jnp.log(3.4)))
    values = jnp.clip(jax.random.normal(first, (K, I, J)), -6.0, 6.0)
    return (values * (rise * spread)[None, :, None]).astype(jnp.float32)


def draw_factor_b(key, part):
    key = jax.random.fold_in(key, 12)
    first, second = jax.random.split(key)
    own = jnp.clip(jax.random.normal(first, (J, R)), -4.0, 4.0)
    shared = jnp.clip(jax.random.normal(second, (J, 1)), -4.0, 4.0)
    return ((own + shared) / jnp.sqrt(J * 1.0)).astype(jnp.float32)


def draw_factor_c(key, part):
    key = jax.random.fold_in(key, 13)
    first, second, third = jax.random.split(key, 3)
    columns = jnp.exp(jax.random.uniform(third, (R,), minval=0.0, maxval=jnp.log(3.0)))
    own = jnp.clip(jax.random.normal(first, (K, R)), -4.0, 4.0)
    shared = jnp.clip(jax.random.normal(second, (K, 1)), -4.0, 4.0)
    return ((own + shared) * columns[None, :] / jnp.sqrt(K * 1.0)).astype(jnp.float32)


def setup_inputs(seed: int = 0) -> dict:
    arg_keys = jax.random.split(jax.random.key(seed), 4)
    tensor = draw_tensor(jax.random.fold_in(arg_keys[3], 71), 0)
    factor_b = draw_factor_b(jax.random.fold_in(arg_keys[3], 71), 0)
    factor_c = draw_factor_c(jax.random.fold_in(arg_keys[3], 71), 0)
    return {"tensor": tensor, "factor_b": factor_b, "factor_c": factor_c}


eps = 1e-06

def reference(tensor, factor_b, factor_c):
    high = lax.Precision.HIGHEST
    gram = jnp.dot(factor_b.T.astype(jnp.float32), factor_b.astype(jnp.float32), precision=high, preferred_element_type=jnp.float32) * jnp.dot(factor_c.T.astype(jnp.float32), factor_c.astype(jnp.float32), precision=high, preferred_element_type=jnp.float32)
    depth, rows_i, cols_j = tensor.shape
    ranks = factor_b.shape[1]

    def frame_step(total, pair):
        slab, weight = pair
        product = jnp.dot(slab.astype(jnp.float32), factor_b.astype(jnp.float32), precision=high, preferred_element_type=jnp.float32)
        return (total + product * weight[None, :], None)
    start = jnp.zeros((rows_i, ranks), jnp.float32)
    mttkrp, unused = lax.scan(frame_step, start, (tensor, factor_c))
    lower = jnp.linalg.cholesky(gram)
    half = lax.linalg.triangular_solve(lower, mttkrp, left_side=False, lower=True, transpose_a=True)
    solved = lax.linalg.triangular_solve(lower, half, left_side=False, lower=True, transpose_a=False)
    col_scale = jnp.sqrt(lax.optimization_barrier(jnp.sum(solved * solved, axis=0)) / rows_i + eps)
    return (solved / col_scale, col_scale)
```

```python
import functools

import jax
import jax.numpy as jnp
from jax import lax
from jax.experimental import pallas as pl
from jax.experimental.pallas import tpu as pltpu
from jax.sharding import PartitionSpec as P

eps = 1e-06
MESH = pl.DeviceIdType.MESH
HIGH = lax.Precision.HIGHEST
TOP = 64
SUB = 8


def push(src, dst, ssem, rsem, device):
    return pltpu.make_async_remote_copy(
        src_ref=src, dst_ref=dst, send_sem=ssem, recv_sem=rsem,
        device_id=device, device_id_type=MESH,
    )


def greet(nr, nc):
    me_r, me_c = lax.axis_index("row"), lax.axis_index("col")
    barrier = pltpu.get_barrier_semaphore()
    for n in range(1, nr):
        pl.semaphore_signal(barrier, inc=1, device_id={"row": lax.rem(me_r + n, nr)}, device_id_type=MESH)
    for n in range(1, nc):
        pl.semaphore_signal(barrier, inc=1, device_id={"col": lax.rem(me_c + n, nc)}, device_id_type=MESH)
    pl.semaphore_wait(barrier, nr + nc - 2)


def nt_dot(a, b, precision=None):
    return lax.dot_general(
        a, b, (((1,), (1,)), ((), ())), precision=precision, preferred_element_type=jnp.float32
    )


def terms_kernel(
    nr, nc, t_ref, b_ref, c_ref, gram_ref, mine_ref,
    bt, bh, bl, gc, gsend, grecv, gfull, msend, mrecv, tbuf,
    tsem, bs, br, gs, gr_, cs, cr, rs, rr, ms, mr,
):
    me_r, me_c = lax.axis_index("row"), lax.axis_index("col")
    depth, share = tbuf.shape[1], tbuf.shape[2]
    rb = b_ref.shape[1]
    rows = gsend.shape[1]
    ranks = bt.shape[0]

    def load(n):
        p = lax.rem(me_c + n, nc)
        start = pl.multiple_of(p * share, share)
        return pltpu.make_async_copy(t_ref.at[:, pl.ds(start, share), :], tbuf.at[n], tsem.at[n])

    for n in list(range(1, nc)) + [0]:
        load(n).start()
    mine_rows = pl.ds(pl.multiple_of(me_r * rb, rb), rb)
    own = b_ref[...].T
    bt[mine_rows, :] = own
    greet(nr, nc)

    copies = []
    for n in range(1, nr):
        copies.append(push(bt.at[mine_rows], bt.at[mine_rows], bs.at[n], br.at[n], {"row": lax.rem(me_r + n, nr)}))
        copies[-1].start()
    c = c_ref[...]
    gc[...] = lax.dot_general(
        c, c, (((0,), (0,)), ((), ())), precision=HIGH, preferred_element_type=jnp.float32
    )
    for n in range(1, nr):
        came = pl.ds(pl.multiple_of(lax.rem(me_r + nr - n, nr) * rb, rb), rb)
        push(bt.at[mine_rows], bt.at[came], bs.at[n], br.at[n], {"row": lax.rem(me_r + n, nr)}).wait_recv()

    full = bt[...]
    part = nt_dot(own, full, HIGH)
    for n in range(nc):
        gsend[n] = part[n * rows:(n + 1) * rows]
    gcopies = []
    for n in range(1, nc):
        p = lax.rem(me_c + n, nc)
        gcopies.append(push(gsend.at[p], grecv.at[n], gs.at[n], gr_.at[n], {"col": p}))
        gcopies[-1].start()
    hi = full.astype(jnp.bfloat16)
    bh[...] = hi
    bl[...] = (full - hi.astype(jnp.float32)).astype(jnp.bfloat16)

    group = max(1, 512 // share)

    def block(n):
        load(n).wait()
        total = jnp.zeros((share, ranks), jnp.float32)
        for g in range(0, depth, group):
            slab = tbuf[n, g:g + group].reshape(group * share, tbuf.shape[3])
            th = slab.astype(jnp.bfloat16)
            tl = (slab - th.astype(jnp.float32)).astype(jnp.bfloat16)
            product = nt_dot(th, bh[...]) + (nt_dot(tl, bh[...]) + nt_dot(th, bl[...]))
            for f in range(group):
                total += product[f * share:(f + 1) * share] * c_ref[g + f:g + f + 1, :]
        msend[n] = total

    def block_send(n):
        return push(msend.at[n], mrecv.at[n], ms.at[n], mr.at[n], {"col": lax.rem(me_c + n, nc)})

    def blocks(first, last):
        @pl.loop(first, last)
        def _(n):
            block(n)
            block_send(n).start()

    cut1, cut2 = nc // 4 + 1, nc // 2 + 1
    blocks(1, cut1)
    for copy in gcopies:
        copy.wait_recv()
    total = gsend[me_c]
    for n in range(1, nc):
        total = total + grecv[n]
    gfull[me_r, me_c] = total
    ccopies = []
    for n in range(1, nc):
        slot = gfull.at[me_r, me_c]
        ccopies.append(push(slot, slot, cs.at[n], cr.at[n], {"col": lax.rem(me_c + n, nc)}))
        ccopies[-1].start()
    blocks(cut1, cut2)
    for n in range(1, nc):
        came = gfull.at[me_r, lax.rem(me_c + nc - n, nc)]
        push(gfull.at[me_r, me_c], came, cs.at[n], cr.at[n], {"col": lax.rem(me_c + n, nc)}).wait_recv()
    rcopies = []
    for n in range(1, nr):
        slot = gfull.at[me_r]
        rcopies.append(push(slot, slot, rs.at[n], rr.at[n], {"row": lax.rem(me_r + n, nr)}))
        rcopies[-1].start()
    blocks(cut2, nc)
    block(0)
    for n in range(1, nr):
        came = gfull.at[lax.rem(me_r + nr - n, nr)]
        push(gfull.at[me_r], came, rs.at[n], rr.at[n], {"row": lax.rem(me_r + n, nr)}).wait_recv()
    for r in range(nr):
        for k in range(nc):
            at = (r * nc + k) * rows
            gram_ref[r, k] = gfull[r, k] * gc[at:at + rows, :]
    total = msend[0]
    for n in range(1, nc):
        block_send(n).wait_recv()
        total = total + mrecv[n]
    mine_ref[...] = total
    for copy in copies + gcopies + ccopies + rcopies:
        copy.wait_send()
    for n in range(1, nc):
        block_send(n).wait_send()


def invert_block(tile, low):
    size = TOP // SUB
    lane = lax.broadcasted_iota(jnp.int32, (SUB, 2 * TOP), 1)
    row = lax.broadcasted_iota(jnp.int32, (SUB, 2 * TOP), 0)
    held = (lane < TOP) if low else (lane >= TOP)
    shift = TOP if low else 0
    base = 0 if low else TOP
    v = []
    for i in range(size):
        unit = (lane == row + (shift + i * SUB)).astype(jnp.float32)
        v.append(jnp.where(held, tile[i * SUB:(i + 1) * SUB], unit))
    wide = (SUB, 2 * TOP)
    for s in range(size):
        cols = [
            [jnp.broadcast_to(v[i][:, base + s * SUB + j:base + s * SUB + j + 1], wide) for j in range(SUB)]
            for i in range(size)
        ]
        head, c = v[s], cols[s]
        for p in range(SUB):
            inv = 1.0 / jnp.broadcast_to(c[p][p:p + 1], wide)
            here = row == p
            pivot = jnp.broadcast_to(head[p:p + 1], wide) * inv
            head = jnp.where(here, pivot, head - c[p] * pivot)
            for j in range(p + 1, SUB):
                q = jnp.broadcast_to(c[j][p:p + 1], wide) * inv
                c[j] = jnp.where(here, q, c[j] - c[p] * q)
        lines = [jnp.broadcast_to(head[j:j + 1], wide) for j in range(SUB)]
        for i in range(size):
            if i == s:
                v[i] = head
            else:
                terms = [cols[i][j] * lines[j] for j in range(SUB)]
                while len(terms) > 1:
                    terms = [a + b for a, b in zip(terms[::2], terms[1::2])]
                v[i] = v[i] - terms[0]
    whole = jnp.concatenate(v, axis=0)
    return whole[:, shift:shift + TOP]


def solve_kernel(gram_ref, mine_ref, solved_ref, squares_ref, a):
    ranks = gram_ref.shape[0]
    share = mine_ref.shape[0]
    a[0:ranks, :] = gram_ref[...]
    a[ranks:, :] = mine_ref[...]
    for b in range(ranks // TOP):
        at = b * TOP
        inverse = invert_block(a[at:at + TOP, (b // 2) * 2 * TOP:(b // 2 + 1) * 2 * TOP], b % 2 == 0)
        below = a[at + TOP:, :]
        w = jnp.dot(below[:, at:at + TOP], inverse, precision=HIGH, preferred_element_type=jnp.float32)
        change = jnp.dot(w, a[at:at + TOP, :], precision=HIGH, preferred_element_type=jnp.float32)
        a[at + TOP:, :] = below - change
        a[at + TOP:, at:at + TOP] = w
    solved = a[ranks:, :]
    solved_ref[...] = solved
    squares_ref[...] = jnp.sum(solved * solved, axis=0, keepdims=True)


def scale_kernel(nr, nc, count, solved_ref, squares_ref, out_ref, scale_ref, first, second, cs, cr, rs, rr):
    me_r, me_c = lax.axis_index("row"), lax.axis_index("col")
    first[me_c] = squares_ref[...]
    greet(nr, nc)
    for buf, me, n_all, ss, sr, name in (
        (first, me_c, nc, cs, cr, "col"), (second, me_r, nr, rs, rr, "row")
    ):
        if name == "row":
            total = first[0]
            for n in range(1, nc):
                total = total + first[n]
            second[me_r] = total
        slot = buf.at[me]
        copies = [
            push(slot, slot, ss.at[n], sr.at[n], {name: lax.rem(me + n, n_all)}) for n in range(1, n_all)
        ]
        for copy in copies:
            copy.start()
        for n in range(1, n_all):
            came = buf.at[lax.rem(me + n_all - n, n_all)]
            push(slot, came, ss.at[n], sr.at[n], {name: lax.rem(me + n, n_all)}).wait_recv()
        for copy in copies:
            copy.wait_send()
    total = second[0]
    for n in range(1, nr):
        total = total + second[n]
    scale = jnp.sqrt(total / count + eps)
    scale_ref[...] = scale
    out_ref[...] = solved_ref[...] / scale


def local(tensor, factor_b, factor_c):
    depth, rows_i, cols_j = tensor.shape
    ranks = factor_c.shape[1]
    rb = factor_b.shape[1]
    nr, nc = lax.axis_size("row"), lax.axis_size("col")
    share = rows_i // nc
    rows = ranks // (nr * nc)
    f32, bf16 = jnp.float32, jnp.bfloat16
    vmem = pl.BlockSpec(memory_space=pltpu.VMEM)
    dma = pltpu.SemaphoreType.DMA
    gram, mine = pl.pallas_call(
        functools.partial(terms_kernel, nr, nc),
        out_shape=(
            jax.ShapeDtypeStruct((nr, nc, rows, ranks), f32),
            jax.ShapeDtypeStruct((share, ranks), f32),
        ),
        in_specs=[pl.BlockSpec(memory_space=pl.ANY), vmem, vmem],
        out_specs=(vmem, vmem),
        scratch_shapes=[
            pltpu.VMEM((ranks, cols_j), f32),
            pltpu.VMEM((ranks, cols_j), bf16),
            pltpu.VMEM((ranks, cols_j), bf16),
            pltpu.VMEM((ranks, ranks), f32),
            pltpu.VMEM((nc, rows, ranks), f32),
            pltpu.VMEM((nc, rows, ranks), f32),
            pltpu.VMEM((nr, nc, rows, ranks), f32),
            pltpu.VMEM((nc, share, ranks), f32),
            pltpu.VMEM((nc, share, ranks), f32),
            pltpu.VMEM((nc, depth, share, cols_j), f32),
            dma((nc,)), dma((nr,)), dma((nr,)), dma((nc,)), dma((nc,)), dma((nc,)), dma((nc,)),
            dma((nr,)), dma((nr,)), dma((nc,)), dma((nc,)),
        ],
        compiler_params=pltpu.CompilerParams(
            collective_id=0, has_side_effects=True, vmem_limit_bytes=40 * 2**20
        ),
        name="terms",
    )(tensor, factor_b, factor_c)
    solved, squares = pl.pallas_call(
        solve_kernel,
        out_shape=(jax.ShapeDtypeStruct((share, ranks), f32), jax.ShapeDtypeStruct((1, ranks), f32)),
        in_specs=[vmem, vmem],
        out_specs=(vmem, vmem),
        scratch_shapes=[pltpu.VMEM((ranks + share, ranks), f32)],
        compiler_params=pltpu.CompilerParams(vmem_limit_bytes=32 * 2**20),
        name="solve",
    )(gram.reshape(ranks, ranks), mine)
    factor_a, col_scale = pl.pallas_call(
        functools.partial(scale_kernel, nr, nc, float(rows_i * nr)),
        out_shape=(jax.ShapeDtypeStruct((share, ranks), f32), jax.ShapeDtypeStruct((1, ranks), f32)),
        in_specs=[vmem, vmem],
        out_specs=(vmem, vmem),
        scratch_shapes=[
            pltpu.VMEM((nc, 1, ranks), f32), pltpu.VMEM((nr, 1, ranks), f32),
            dma((nc,)), dma((nc,)), dma((nr,)), dma((nr,)),
        ],
        compiler_params=pltpu.CompilerParams(collective_id=1, has_side_effects=True),
        name="scale",
    )(solved, squares)
    return (factor_a, col_scale.reshape(ranks))


def solution(mesh):
    return jax.shard_map(
        local,
        mesh=mesh,
        in_specs=(P(None, "row", "col"), P("col", "row"), P()),
        out_specs=(P(("row", "col"), None), P()),
        check_vma=False,
    )
```

```python
import functools

import jax
import jax.numpy as jnp
from jax import lax
from jax.experimental import pallas as pl
from jax.experimental.pallas import tpu as pltpu
from jax.sharding import PartitionSpec as P

eps = 1e-06
MESH = pl.DeviceIdType.MESH
HIGH = lax.Precision.HIGHEST
TOP = 64
SUB = 8


def push(src, dst, ssem, rsem, device):
    return pltpu.make_async_remote_copy(
        src_ref=src, dst_ref=dst, send_sem=ssem, recv_sem=rsem,
        device_id=device, device_id_type=MESH,
    )


def greet(nr, nc):
    me_r, me_c = lax.axis_index("row"), lax.axis_index("col")
    barrier = pltpu.get_barrier_semaphore()
    for n in range(1, nr):
        pl.semaphore_signal(barrier, inc=1, device_id={"row": lax.rem(me_r + n, nr)}, device_id_type=MESH)
    for n in range(1, nc):
        pl.semaphore_signal(barrier, inc=1, device_id={"col": lax.rem(me_c + n, nc)}, device_id_type=MESH)
    return lambda: pl.semaphore_wait(barrier, nr + nc - 2)


def nt_dot(a, b, precision=None):
    return lax.dot_general(
        a, b, (((1,), (1,)), ((), ())), precision=precision, preferred_element_type=jnp.float32
    )


def invert_block(tile, low):
    size = TOP // SUB
    lane = lax.broadcasted_iota(jnp.int32, (SUB, 2 * TOP), 1)
    row = lax.broadcasted_iota(jnp.int32, (SUB, 2 * TOP), 0)
    held = (lane < TOP) if low else (lane >= TOP)
    shift = TOP if low else 0
    base = 0 if low else TOP
    v = []
    for i in range(size):
        unit = (lane == row + (shift + i * SUB)).astype(jnp.float32)
        v.append(jnp.where(held, tile[i * SUB:(i + 1) * SUB], unit))
    wide = (SUB, 2 * TOP)
    for s in range(size):
        cols = [
            [jnp.broadcast_to(v[i][:, base + s * SUB + j:base + s * SUB + j + 1], wide) for j in range(SUB)]
            for i in range(size)
        ]
        head, c = v[s], cols[s]
        for p in range(SUB):
            inv = 1.0 / jnp.broadcast_to(c[p][p:p + 1], wide)
            here = row == p
            pivot = jnp.broadcast_to(head[p:p + 1], wide) * inv
            head = jnp.where(here, pivot, head - c[p] * pivot)
            for j in range(p + 1, SUB):
                q = jnp.broadcast_to(c[j][p:p + 1], wide) * inv
                c[j] = jnp.where(here, q, c[j] - c[p] * q)
        lines = [jnp.broadcast_to(head[j:j + 1], wide) for j in range(SUB)]
        for i in range(size):
            if i == s:
                v[i] = head
            else:
                terms = [cols[i][j] * lines[j] for j in range(SUB)]
                while len(terms) > 1:
                    terms = [a + b for a, b in zip(terms[::2], terms[1::2])]
                v[i] = v[i] - terms[0]
    whole = jnp.concatenate(v, axis=0)
    return whole[:, shift:shift + TOP]


def whole_kernel(
    nr, nc, t_ref, b_hbm, c_hbm, solved_ref, squares_ref,
    bt, bcat, gc, gsend, grecv, gfull, msend, mrecv, tbuf, c_ref, a, first, second,
    tsem, lsem, bs, br, gs, gr_, cs, cr, rs, rr, ms, mr, qs, qr, us, ur,
):
    me_r, me_c = lax.axis_index("row"), lax.axis_index("col")
    depth, share = tbuf.shape[1], tbuf.shape[2]
    rb = b_hbm.shape[0]
    rows = gsend.shape[1]
    ranks = bt.shape[0]

    def load(n):
        p = lax.rem(me_c + n, nc)
        start = pl.multiple_of(p * share, share)
        return pltpu.make_async_copy(t_ref.at[:, pl.ds(start, share), :], tbuf.at[n], tsem.at[n])

    greeted = greet(nr, nc)
    mine_rows = pl.ds(pl.multiple_of(me_r * rb, rb), rb)
    own_copy = pltpu.make_async_copy(b_hbm, bt.at[mine_rows], lsem.at[0])
    c_copy = pltpu.make_async_copy(c_hbm, c_ref, lsem.at[1])
    own_copy.start()
    c_copy.start()
    for n in list(range(1, nc)) + [0]:
        load(n).start()
    greeted()

    copies = []
    for n in range(1, nr):
        copies.append(push(b_hbm, bt.at[mine_rows], bs.at[n], br.at[n], {"row": lax.rem(me_r + n, nr)}))
        copies[-1].start()
    c_copy.wait()
    c = c_ref[...]
    gc[...] = lax.dot_general(
        c, c, (((0,), (0,)), ((), ())), precision=HIGH, preferred_element_type=jnp.float32
    )
    for n in range(1, nr):
        came = pl.ds(pl.multiple_of(lax.rem(me_r + nr - n, nr) * rb, rb), rb)
        push(b_hbm, bt.at[came], bs.at[n], br.at[n], {"row": lax.rem(me_r + n, nr)}).wait_recv()

    own_copy.wait()
    full = bt[...]
    own = bt[mine_rows, :]
    part = nt_dot(own, full, HIGH)
    for n in range(nc):
        gsend[n] = part[n * rows:(n + 1) * rows]
    gcopies = []
    for n in range(1, nc):
        p = lax.rem(me_c + n, nc)
        gcopies.append(push(gsend.at[p], grecv.at[n], gs.at[n], gr_.at[n], {"col": p}))
        gcopies[-1].start()
    hi = full.astype(jnp.bfloat16)
    lo = (full - hi.astype(jnp.float32)).astype(jnp.bfloat16)
    bcat[...] = jnp.concatenate([hi, hi, lo], axis=1)

    group = max(1, 512 // share)

    def block(n):
        load(n).wait()
        total = jnp.zeros((share, ranks), jnp.float32)
        for g in range(0, depth, group):
            slab = tbuf[n, g:g + group].reshape(group * share, tbuf.shape[3])
            th = slab.astype(jnp.bfloat16)
            tl = (slab - th.astype(jnp.float32)).astype(jnp.bfloat16)
            product = nt_dot(jnp.concatenate([th, tl, th], axis=1), bcat[...])
            for f in range(group):
                total += product[f * share:(f + 1) * share] * c_ref[g + f:g + f + 1, :]
        msend[n] = total

    def block_send(n):
        return push(msend.at[n], mrecv.at[n], ms.at[n], mr.at[n], {"col": lax.rem(me_c + n, nc)})

    def blocks(first, last):
        @pl.loop(first, last)
        def _(n):
            block(n)
            block_send(n).start()

    cut1, cut2 = nc // 4 + 1, nc // 2 + 1
    blocks(1, cut1)
    for copy in gcopies:
        copy.wait_recv()
    total = gsend[me_c]
    for n in range(1, nc):
        total = total + grecv[n]
    gfull[me_r, me_c] = total
    ccopies = []
    for n in range(1, nc):
        slot = gfull.at[me_r, me_c]
        ccopies.append(push(slot, slot, cs.at[n], cr.at[n], {"col": lax.rem(me_c + n, nc)}))
        ccopies[-1].start()
    blocks(cut1, cut2)
    for n in range(1, nc):
        came = gfull.at[me_r, lax.rem(me_c + nc - n, nc)]
        push(gfull.at[me_r, me_c], came, cs.at[n], cr.at[n], {"col": lax.rem(me_c + n, nc)}).wait_recv()
    rcopies = []
    for n in range(1, nr):
        slot = gfull.at[me_r]
        rcopies.append(push(slot, slot, rs.at[n], rr.at[n], {"row": lax.rem(me_r + n, nr)}))
        rcopies[-1].start()
    blocks(cut2, nc)
    block(0)
    for n in range(1, nr):
        came = gfull.at[lax.rem(me_r + nr - n, nr)]
        push(gfull.at[me_r], came, rs.at[n], rr.at[n], {"row": lax.rem(me_r + n, nr)}).wait_recv()
    for r in range(nr):
        for k in range(nc):
            at = (r * nc + k) * rows
            a[at:at + rows, :] = gfull[r, k] * gc[at:at + rows, :]

    for b in range(ranks // TOP):
        at = b * TOP
        inverse = invert_block(a[at:at + TOP, (b // 2) * 2 * TOP:(b // 2 + 1) * 2 * TOP], b % 2 == 0)
        if b == 0:
            total = msend[0]
            for n in range(1, nc):
                block_send(n).wait_recv()
                total = total + mrecv[n]
            a[ranks:, :] = total
        below = a[at + TOP:, :]
        w = jnp.dot(below[:, at:at + TOP], inverse, precision=HIGH, preferred_element_type=jnp.float32)
        change = jnp.dot(w, a[at:at + TOP, :], precision=HIGH, preferred_element_type=jnp.float32)
        a[at + TOP:, :] = below - change
        a[at + TOP:, at:at + TOP] = w
    solved = a[ranks:, :]
    first[me_c] = jnp.sum(solved * solved, axis=0, keepdims=True)
    for buf, me, n_all, ss, sr, name in (
        (first, me_c, nc, qs, qr, "col"), (second, me_r, nr, us, ur, "row")
    ):
        if name == "row":
            total = first[0]
            for n in range(1, nc):
                total = total + first[n]
            second[me_r] = total
        slot = buf.at[me]
        copies += [
            push(slot, slot, ss.at[n], sr.at[n], {name: lax.rem(me + n, n_all)}) for n in range(1, n_all)
        ]
        for copy in copies[1 - n_all:]:
            copy.start()
        if name == "col":
            solved_ref[...] = solved
        for n in range(1, n_all):
            came = buf.at[lax.rem(me + n_all - n, n_all)]
            push(slot, came, ss.at[n], sr.at[n], {name: lax.rem(me + n, n_all)}).wait_recv()
    total = second[0]
    for n in range(1, nr):
        total = total + second[n]
    squares_ref[...] = total
    for copy in copies + gcopies + ccopies + rcopies:
        copy.wait_send()
    for n in range(1, nc):
        block_send(n).wait_send()


def local(tensor, factor_b, factor_c):
    depth, rows_i, cols_j = tensor.shape
    ranks = factor_c.shape[1]
    nr, nc = lax.axis_size("row"), lax.axis_size("col")
    share = rows_i // nc
    rows = ranks // (nr * nc)
    f32, bf16 = jnp.float32, jnp.bfloat16
    vmem = pl.BlockSpec(memory_space=pltpu.VMEM)
    hbm = pl.BlockSpec(memory_space=pl.ANY)
    dma = pltpu.SemaphoreType.DMA
    solved, squares = pl.pallas_call(
        functools.partial(whole_kernel, nr, nc),
        out_shape=(jax.ShapeDtypeStruct((share, ranks), f32), jax.ShapeDtypeStruct((1, ranks), f32)),
        in_specs=[hbm, hbm, hbm],
        out_specs=(vmem, vmem),
        scratch_shapes=[
            pltpu.VMEM((ranks, cols_j), f32),
            pltpu.VMEM((ranks, 3 * cols_j), bf16),
            pltpu.VMEM((ranks, ranks), f32),
            pltpu.VMEM((nc, rows, ranks), f32),
            pltpu.VMEM((nc, rows, ranks), f32),
            pltpu.VMEM((nr, nc, rows, ranks), f32),
            pltpu.VMEM((nc, share, ranks), f32),
            pltpu.VMEM((nc, share, ranks), f32),
            pltpu.VMEM((nc, depth, share, cols_j), f32),
            pltpu.VMEM((depth, ranks), f32),
            pltpu.VMEM((ranks + share, ranks), f32),
            pltpu.VMEM((nc, 1, ranks), f32),
            pltpu.VMEM((nr, 1, ranks), f32),
            dma((nc,)), dma((2,)), dma((nr,)), dma((nr,)), dma((nc,)), dma((nc,)), dma((nc,)), dma((nc,)),
            dma((nr,)), dma((nr,)), dma((nc,)), dma((nc,)), dma((nc,)), dma((nc,)), dma((nr,)), dma((nr,)),
        ],
        compiler_params=pltpu.CompilerParams(
            collective_id=0, has_side_effects=True, vmem_limit_bytes=40 * 2**20
        ),
        name="whole",
    )(tensor, factor_b.T, factor_c)
    col_scale = jnp.sqrt(squares / (rows_i * nr) + eps)
    return (solved / col_scale, col_scale.reshape(ranks))


def solution(mesh):
    return jax.shard_map(
        local,
        mesh=mesh,
        in_specs=(P(None, "row", "col"), P("col", "row"), P()),
        out_specs=(P(("row", "col"), None), P()),
        check_vma=False,
    )
```

```python
import functools

import jax
import jax.numpy as jnp
from jax import lax
from jax.experimental import pallas as pl
from jax.experimental.pallas import tpu as pltpu
from jax.sharding import PartitionSpec as P

eps = 1e-06
MESH = pl.DeviceIdType.MESH
HIGH = lax.Precision.HIGHEST
TOP = 64
SUB = 8


def push(src, dst, ssem, rsem, device):
    return pltpu.make_async_remote_copy(
        src_ref=src, dst_ref=dst, send_sem=ssem, recv_sem=rsem,
        device_id=device, device_id_type=MESH,
    )


def greet(nr, nc):
    me_r, me_c = lax.axis_index("row"), lax.axis_index("col")
    barrier = pltpu.get_barrier_semaphore()
    for n in range(1, nr):
        pl.semaphore_signal(barrier, inc=1, device_id={"row": lax.rem(me_r + n, nr)}, device_id_type=MESH)
    for n in range(1, nc):
        pl.semaphore_signal(barrier, inc=1, device_id={"col": lax.rem(me_c + n, nc)}, device_id_type=MESH)
    return lambda: pl.semaphore_wait(barrier, nr + nc - 2)


def nt_dot(a, b, precision=None):
    return lax.dot_general(
        a, b, (((1,), (1,)), ((), ())), precision=precision, preferred_element_type=jnp.float32
    )


def line(held, p):
    return jnp.broadcast_to(held[p:p + 1], held.shape)


def invert_block(tile, low):
    size = TOP // SUB
    lane = lax.broadcasted_iota(jnp.int32, (SUB, 2 * TOP), 1)
    row = lax.broadcasted_iota(jnp.int32, (SUB, 2 * TOP), 0)
    held = (lane < TOP) if low else (lane >= TOP)
    shift = TOP if low else 0
    base = 0 if low else TOP
    v = []
    for i in range(size):
        unit = (lane == row + (shift + i * SUB)).astype(jnp.float32)
        v.append(jnp.where(held, tile[i * SUB:(i + 1) * SUB], unit))
    wide = (SUB, 2 * TOP)
    for s in range(size):
        cols = [
            [jnp.broadcast_to(v[i][:, base + s * SUB + j:base + s * SUB + j + 1], wide) for j in range(SUB)]
            for i in range(size)
        ]
        head, c = v[s], list(cols[s])
        for p in range(0, SUB, 2):
            cp, cq = c[p], c[p + 1]
            first, second = row == p, row == p + 1
            here = first | second
            a, d = line(cp, p), line(cq, p + 1)
            b, e = line(cq, p), line(cp, p + 1)
            inv = 1.0 / (a * d - b * e)
            cp = jnp.where(first, -1.0, jnp.where(second, 0.0, cp))
            cq = jnp.where(second, -1.0, jnp.where(first, 0.0, cq))

            def step(held):
                x, y = line(held, p), line(held, p + 1)
                change = cp * (d * x - b * y) + cq * (a * y - e * x)
                return jnp.where(here, 0.0, held) - change * inv

            for j in range(p + 2, SUB):
                c[j] = step(c[j])
            head = step(head)
        lines = [line(head, j) for j in range(SUB)]
        for i in range(size):
            if i == s:
                v[i] = head
            else:
                terms = [cols[i][j] * lines[j] for j in range(SUB)]
                while len(terms) > 1:
                    terms = [a + b for a, b in zip(terms[::2], terms[1::2])]
                v[i] = v[i] - terms[0]
    whole = jnp.concatenate(v, axis=0)
    return whole[:, shift:shift + TOP]


def whole_kernel(
    nr, nc, t_ref, b_hbm, c_hbm, solved_ref, squares_ref,
    bt, bcat, gc, gsend, grecv, gfull, msend, mrecv, tbuf, c_ref, a, first, second,
    tsem, lsem, bs, br, gs, gr_, cs, cr, rs, rr, ms, mr, qs, qr, us, ur,
):
    me_r, me_c = lax.axis_index("row"), lax.axis_index("col")
    depth, share = tbuf.shape[1], tbuf.shape[2]
    rb = b_hbm.shape[0]
    rows = gsend.shape[1]
    ranks = bt.shape[0]

    def load(n):
        p = lax.rem(me_c + n, nc)
        start = pl.multiple_of(p * share, share)
        return pltpu.make_async_copy(t_ref.at[:, pl.ds(start, share), :], tbuf.at[n], tsem.at[n])

    greeted = greet(nr, nc)
    mine_rows = pl.ds(pl.multiple_of(me_r * rb, rb), rb)
    own_copy = pltpu.make_async_copy(b_hbm, bt.at[mine_rows], lsem.at[0])
    c_copy = pltpu.make_async_copy(c_hbm, c_ref, lsem.at[1])
    own_copy.start()
    c_copy.start()
    for n in list(range(1, nc)) + [0]:
        load(n).start()
    greeted()

    copies = []
    for n in range(1, nr):
        copies.append(push(b_hbm, bt.at[mine_rows], bs.at[n], br.at[n], {"row": lax.rem(me_r + n, nr)}))
        copies[-1].start()
    c_copy.wait()
    c = c_ref[...]
    gc[...] = lax.dot_general(
        c, c, (((0,), (0,)), ((), ())), precision=HIGH, preferred_element_type=jnp.float32
    )
    for n in range(1, nr):
        came = pl.ds(pl.multiple_of(lax.rem(me_r + nr - n, nr) * rb, rb), rb)
        push(b_hbm, bt.at[came], bs.at[n], br.at[n], {"row": lax.rem(me_r + n, nr)}).wait_recv()

    own_copy.wait()
    full = bt[...]
    own = bt[mine_rows, :]
    part = nt_dot(own, full, HIGH)
    for n in range(nc):
        gsend[n] = part[n * rows:(n + 1) * rows]
    gcopies = []
    for n in range(1, nc):
        p = lax.rem(me_c + n, nc)
        gcopies.append(push(gsend.at[p], grecv.at[n], gs.at[n], gr_.at[n], {"col": p}))
        gcopies[-1].start()
    turned = full.T
    hi = turned.astype(jnp.bfloat16)
    lo = (turned - hi.astype(jnp.float32)).astype(jnp.bfloat16)
    bcat[...] = jnp.concatenate([hi, hi, lo], axis=0)

    group = max(1, 512 // share)

    def block(n):
        load(n).wait()
        total = jnp.zeros((share, ranks), jnp.float32)
        for g in range(0, depth, group):
            slab = tbuf[n, g:g + group].reshape(group * share, tbuf.shape[3])
            th = slab.astype(jnp.bfloat16)
            tl = (slab - th.astype(jnp.float32)).astype(jnp.bfloat16)
            product = jnp.dot(
                jnp.concatenate([th, tl, th], axis=1), bcat[...], preferred_element_type=jnp.float32
            )
            for f in range(group):
                total += product[f * share:(f + 1) * share] * c_ref[g + f:g + f + 1, :]
        msend[n] = total

    def block_send(n):
        return push(msend.at[n], mrecv.at[n], ms.at[n], mr.at[n], {"col": lax.rem(me_c + n, nc)})

    def blocks(first, last):
        @pl.loop(first, last)
        def _(n):
            block(n)
            block_send(n).start()

    cut1, cut2 = nc // 4 + 1, nc // 2 + 1
    blocks(1, cut1)
    for copy in gcopies:
        copy.wait_recv()
    total = gsend[me_c]
    for n in range(1, nc):
        total = total + grecv[n]
    gfull[me_r, me_c] = total
    ccopies = []
    for n in range(1, nc):
        slot = gfull.at[me_r, me_c]
        ccopies.append(push(slot, slot, cs.at[n], cr.at[n], {"col": lax.rem(me_c + n, nc)}))
        ccopies[-1].start()
    blocks(cut1, cut2)
    for n in range(1, nc):
        came = gfull.at[me_r, lax.rem(me_c + nc - n, nc)]
        push(gfull.at[me_r, me_c], came, cs.at[n], cr.at[n], {"col": lax.rem(me_c + n, nc)}).wait_recv()
    rcopies = []
    for n in range(1, nr):
        slot = gfull.at[me_r]
        rcopies.append(push(slot, slot, rs.at[n], rr.at[n], {"row": lax.rem(me_r + n, nr)}))
        rcopies[-1].start()
    blocks(cut2, nc)
    block(0)
    for n in range(1, nr):
        came = gfull.at[lax.rem(me_r + nr - n, nr)]
        push(gfull.at[me_r], came, rs.at[n], rr.at[n], {"row": lax.rem(me_r + n, nr)}).wait_recv()
    lanes = lax.broadcasted_iota(jnp.int32, (rows, ranks), 1)
    subs = lax.broadcasted_iota(jnp.int32, (rows, ranks), 0)
    diagonal = jnp.zeros((rows, ranks), jnp.float32)
    for r in range(nr):
        for k in range(nc):
            at = (r * nc + k) * rows
            held = gfull[r, k] * gc[at:at + rows, :]
            a[at:at + rows, :] = held
            diagonal = jnp.where(lanes == subs + at, held, diagonal)
    unit = 1.0 / jnp.sum(diagonal, axis=0, keepdims=True)
    a[0:ranks, :] = a[0:ranks, :] * unit

    def inverted(b):
        at = b * TOP
        return invert_block(a[at:at + TOP, (b // 2) * 2 * TOP:(b // 2 + 1) * 2 * TOP], b % 2 == 0)

    def update(low, high, at, inverse):
        held = a[low:high, :]
        w = jnp.dot(held[:, at:at + TOP], inverse, precision=HIGH, preferred_element_type=jnp.float32)
        change = jnp.dot(w, a[at:at + TOP, :], precision=HIGH, preferred_element_type=jnp.float32)
        a[low:high, :] = held - change
        a[low:high, at:at + TOP] = w

    inverse = inverted(0)
    total = msend[0]
    for n in range(1, nc):
        block_send(n).wait_recv()
        total = total + mrecv[n]
    a[ranks:, :] = total * unit
    for at in range(0, ranks, TOP):
        low, high = at + TOP, a.shape[0]
        if low < ranks:
            update(low, low + TOP, at, inverse)
            later = inverted(low // TOP)
            update(low + TOP, high, at, inverse)
            inverse = later
        else:
            update(low, high, at, inverse)
    solved = a[ranks:, :]
    first[me_c] = jnp.sum(solved * solved, axis=0, keepdims=True)
    for buf, me, n_all, ss, sr, name in (
        (first, me_c, nc, qs, qr, "col"), (second, me_r, nr, us, ur, "row")
    ):
        if name == "row":
            total = first[0]
            for n in range(1, nc):
                total = total + first[n]
            second[me_r] = total
        slot = buf.at[me]
        copies += [
            push(slot, slot, ss.at[n], sr.at[n], {name: lax.rem(me + n, n_all)}) for n in range(1, n_all)
        ]
        for copy in copies[1 - n_all:]:
            copy.start()
        if name == "col":
            solved_ref[...] = solved
        for n in range(1, n_all):
            came = buf.at[lax.rem(me + n_all - n, n_all)]
            push(slot, came, ss.at[n], sr.at[n], {name: lax.rem(me + n, n_all)}).wait_recv()
    total = second[0]
    for n in range(1, nr):
        total = total + second[n]
    squares_ref[...] = total
    for copy in copies + gcopies + ccopies + rcopies:
        copy.wait_send()
    for n in range(1, nc):
        block_send(n).wait_send()


def local(tensor, factor_b, factor_c):
    depth, rows_i, cols_j = tensor.shape
    ranks = factor_c.shape[1]
    nr, nc = lax.axis_size("row"), lax.axis_size("col")
    share = rows_i // nc
    rows = ranks // (nr * nc)
    f32, bf16 = jnp.float32, jnp.bfloat16
    vmem = pl.BlockSpec(memory_space=pltpu.VMEM)
    hbm = pl.BlockSpec(memory_space=pltpu.HBM)
    dma = pltpu.SemaphoreType.DMA
    solved, squares = pl.pallas_call(
        functools.partial(whole_kernel, nr, nc),
        out_shape=(jax.ShapeDtypeStruct((share, ranks), f32), jax.ShapeDtypeStruct((1, ranks), f32)),
        in_specs=[hbm, hbm, hbm],
        out_specs=(vmem, vmem),
        scratch_shapes=[
            pltpu.VMEM((ranks, cols_j), f32),
            pltpu.VMEM((3 * cols_j, ranks), bf16),
            pltpu.VMEM((ranks, ranks), f32),
            pltpu.VMEM((nc, rows, ranks), f32),
            pltpu.VMEM((nc, rows, ranks), f32),
            pltpu.VMEM((nr, nc, rows, ranks), f32),
            pltpu.VMEM((nc, share, ranks), f32),
            pltpu.VMEM((nc, share, ranks), f32),
            pltpu.VMEM((nc, depth, share, cols_j), f32),
            pltpu.VMEM((depth, ranks), f32),
            pltpu.VMEM((ranks + share, ranks), f32),
            pltpu.VMEM((nc, 1, ranks), f32),
            pltpu.VMEM((nr, 1, ranks), f32),
            dma((nc,)), dma((2,)), dma((nr,)), dma((nr,)), dma((nc,)), dma((nc,)), dma((nc,)), dma((nc,)),
            dma((nr,)), dma((nr,)), dma((nc,)), dma((nc,)), dma((nc,)), dma((nc,)), dma((nr,)), dma((nr,)),
        ],
        compiler_params=pltpu.CompilerParams(
            collective_id=0, has_side_effects=True, vmem_limit_bytes=40 * 2**20
        ),
        name="whole",
    )(tensor, factor_b.T, factor_c)
    col_scale = jnp.sqrt(squares / (rows_i * nr) + eps)
    return (solved / col_scale, col_scale.reshape(ranks))


def solution(mesh):
    return jax.shard_map(
        local,
        mesh=mesh,
        in_specs=(P(None, "row", "col"), P("col", "row"), P()),
        out_specs=(P(("row", "col"), None), P()),
        check_vma=False,
    )
```

```python
import functools

import jax
import jax.numpy as jnp
from jax import lax
from jax.experimental import pallas as pl
from jax.experimental.pallas import tpu as pltpu
from jax.sharding import PartitionSpec as P

eps = 1e-06
MESH = pl.DeviceIdType.MESH
HIGH = lax.Precision.HIGHEST
TOP = 64
SUB = 8


def push(src, dst, ssem, rsem, device):
    return pltpu.make_async_remote_copy(
        src_ref=src, dst_ref=dst, send_sem=ssem, recv_sem=rsem,
        device_id=device, device_id_type=MESH,
    )


def greet(nr, nc):
    me_r, me_c = lax.axis_index("row"), lax.axis_index("col")
    barrier = pltpu.get_barrier_semaphore()
    for n in range(1, nr):
        pl.semaphore_signal(barrier, inc=1, device_id={"row": lax.rem(me_r + n, nr)}, device_id_type=MESH)
    for n in range(1, nc):
        pl.semaphore_signal(barrier, inc=1, device_id={"col": lax.rem(me_c + n, nc)}, device_id_type=MESH)
    return lambda: pl.semaphore_wait(barrier, nr + nc - 2)


def nt_dot(a, b, precision=None):
    return lax.dot_general(
        a, b, (((1,), (1,)), ((), ())), precision=precision, preferred_element_type=jnp.float32
    )


def line(held, p):
    return jnp.broadcast_to(held[p:p + 1], held.shape)


def invert_block(tile, low):
    size = TOP // SUB
    lane = lax.broadcasted_iota(jnp.int32, (SUB, 2 * TOP), 1)
    row = lax.broadcasted_iota(jnp.int32, (SUB, 2 * TOP), 0)
    held = (lane < TOP) if low else (lane >= TOP)
    shift = TOP if low else 0
    base = 0 if low else TOP
    v = []
    for i in range(size):
        unit = (lane == row + (shift + i * SUB)).astype(jnp.float32)
        v.append(jnp.where(held, tile[i * SUB:(i + 1) * SUB], unit))
    wide = (SUB, 2 * TOP)
    for s in range(size):
        cols = [
            [jnp.broadcast_to(v[i][:, base + s * SUB + j:base + s * SUB + j + 1], wide) for j in range(SUB)]
            for i in range(size)
        ]
        head, c = v[s], list(cols[s])
        for p in range(0, SUB, 2):
            cp, cq = c[p], c[p + 1]
            first, second = row == p, row == p + 1
            here = first | second
            a, d = line(cp, p), line(cq, p + 1)
            b, e = line(cq, p), line(cp, p + 1)
            inv = pl.reciprocal(a * d - b * e, approx=True)
            cp = jnp.where(first, -1.0, jnp.where(second, 0.0, cp))
            cq = jnp.where(second, -1.0, jnp.where(first, 0.0, cq))

            def step(held):
                x, y = line(held, p), line(held, p + 1)
                change = cp * (d * x - b * y) + cq * (a * y - e * x)
                return jnp.where(here, 0.0, held) - change * inv

            for j in range(p + 2, SUB):
                c[j] = step(c[j])
            head = step(head)
        lines = [line(head, j) for j in range(SUB)]
        for i in range(size):
            if i == s:
                v[i] = head
            else:
                terms = [cols[i][j] * lines[j] for j in range(SUB)]
                while len(terms) > 1:
                    terms = [a + b for a, b in zip(terms[::2], terms[1::2])]
                v[i] = v[i] - terms[0]
    whole = jnp.concatenate(v, axis=0)
    return whole[:, shift:shift + TOP]


def whole_kernel(
    nr, nc, t_ref, b_hbm, c_hbm, solved_ref, squares_ref,
    bt, bcat, gc, gsend, grecv, gfull, msend, mrecv, tbuf, tcat, c_ref, a, parts,
    tsem, lsem, bs, br, gs, gr_, cs, cr, rs, rr, ms, mr, qs, qr,
):
    me_r, me_c = lax.axis_index("row"), lax.axis_index("col")
    depth, share = tbuf.shape[1], tbuf.shape[2]
    rb = b_hbm.shape[0]
    rows = gsend.shape[1]
    ranks = bt.shape[0]

    def load(n):
        p = lax.rem(me_c + n, nc)
        start = pl.multiple_of(p * share, share)
        return pltpu.make_async_copy(t_ref.at[:, pl.ds(start, share), :], tbuf.at[n], tsem.at[n])

    greeted = greet(nr, nc)
    mine_rows = pl.ds(pl.multiple_of(me_r * rb, rb), rb)
    own_copy = pltpu.make_async_copy(b_hbm, bt.at[mine_rows], lsem.at[0])
    c_copy = pltpu.make_async_copy(c_hbm, c_ref, lsem.at[1])
    own_copy.start()
    c_copy.start()
    for n in list(range(1, nc)) + [0]:
        load(n).start()
    greeted()

    copies = []
    for n in range(1, nr):
        copies.append(push(b_hbm, bt.at[mine_rows], bs.at[n], br.at[n], {"row": lax.rem(me_r + n, nr)}))
        copies[-1].start()
    c_copy.wait()
    c = c_ref[...]
    gc[...] = lax.dot_general(
        c, c, (((0,), (0,)), ((), ())), precision=HIGH, preferred_element_type=jnp.float32
    )
    group = max(1, 512 // share)
    wide = tbuf.shape[3]

    @pl.loop(1, nc + 1)
    def _(step):
        n = lax.rem(step, nc)
        load(n).wait()
        for g in range(0, depth, group):
            slab = tbuf[n, g:g + group].reshape(group * share, wide)
            th = slab.astype(jnp.bfloat16)
            tcat[n, g * share:(g + group) * share, :wide] = th
            tcat[n, g * share:(g + group) * share, wide:] = (slab - th.astype(jnp.float32)).astype(jnp.bfloat16)

    for n in range(1, nr):
        came = pl.ds(pl.multiple_of(lax.rem(me_r + nr - n, nr) * rb, rb), rb)
        push(b_hbm, bt.at[came], bs.at[n], br.at[n], {"row": lax.rem(me_r + n, nr)}).wait_recv()

    own_copy.wait()
    full = bt[...]
    own = bt[mine_rows, :]
    part = nt_dot(own, full, HIGH)
    for n in range(nc):
        gsend[n] = part[n * rows:(n + 1) * rows]
    gcopies = []
    for n in range(1, nc):
        p = lax.rem(me_c + n, nc)
        gcopies.append(push(gsend.at[p], grecv.at[n], gs.at[n], gr_.at[n], {"col": p}))
        gcopies[-1].start()
    turned = full.T
    hi = turned.astype(jnp.bfloat16)
    lo = (turned - hi.astype(jnp.float32)).astype(jnp.bfloat16)
    bcat[...] = jnp.concatenate([hi, hi, lo], axis=0)

    def block(n):
        total = jnp.zeros((share, ranks), jnp.float32)
        for g in range(0, depth, group):
            halves = tcat[n, g * share:(g + group) * share, :]
            product = jnp.dot(
                jnp.concatenate([halves, halves[:, :wide]], axis=1), bcat[...], preferred_element_type=jnp.float32
            )
            for f in range(group):
                total += product[f * share:(f + 1) * share] * c_ref[g + f:g + f + 1, :]
        msend[n] = total

    def block_send(n):
        return push(msend.at[n], mrecv.at[n], ms.at[n], mr.at[n], {"col": lax.rem(me_c + n, nc)})

    def blocks(first, last):
        @pl.loop(first, last)
        def _(n):
            block(n)
            block_send(n).start()

    cut1, cut2 = nc // 4 + 1, nc // 2 + 1
    blocks(1, cut1)
    for copy in gcopies:
        copy.wait_recv()
    total = gsend[me_c]
    for n in range(1, nc):
        total = total + grecv[n]
    gfull[me_r, me_c] = total
    ccopies = []
    for n in range(1, nc):
        slot = gfull.at[me_r, me_c]
        ccopies.append(push(slot, slot, cs.at[n], cr.at[n], {"col": lax.rem(me_c + n, nc)}))
        ccopies[-1].start()
    blocks(cut1, cut2)
    for n in range(1, nc):
        came = gfull.at[me_r, lax.rem(me_c + nc - n, nc)]
        push(gfull.at[me_r, me_c], came, cs.at[n], cr.at[n], {"col": lax.rem(me_c + n, nc)}).wait_recv()
    rcopies = []
    for n in range(1, nr):
        slot = gfull.at[me_r]
        rcopies.append(push(slot, slot, rs.at[n], rr.at[n], {"row": lax.rem(me_r + n, nr)}))
        rcopies[-1].start()
    blocks(cut2, nc)
    block(0)
    for n in range(1, nr):
        came = gfull.at[lax.rem(me_r + nr - n, nr)]
        push(gfull.at[me_r], came, rs.at[n], rr.at[n], {"row": lax.rem(me_r + n, nr)}).wait_recv()
    lanes = lax.broadcasted_iota(jnp.int32, (rows, ranks), 1)
    subs = lax.broadcasted_iota(jnp.int32, (rows, ranks), 0)
    diagonal = jnp.zeros((rows, ranks), jnp.float32)
    for r in range(nr):
        for k in range(nc):
            at = (r * nc + k) * rows
            held = gfull[r, k] * gc[at:at + rows, :]
            a[at:at + rows, :] = held
            diagonal = jnp.where(lanes == subs + at, held, diagonal)
    unit = 1.0 / jnp.sum(diagonal, axis=0, keepdims=True)
    a[0:ranks, :] = a[0:ranks, :] * unit

    def inverted(b):
        at = b * TOP
        return invert_block(a[at:at + TOP, (b // 2) * 2 * TOP:(b // 2 + 1) * 2 * TOP], b % 2 == 0)

    def update(low, high, at, inverse):
        held = a[low:high, :]
        w = jnp.dot(held[:, at:at + TOP], inverse, precision=HIGH, preferred_element_type=jnp.float32)
        change = jnp.dot(w, a[at:at + TOP, :], precision=HIGH, preferred_element_type=jnp.float32)
        a[low:high, :] = held - change
        a[low:high, at:at + TOP] = w

    inverse = inverted(0)
    total = msend[0]
    for n in range(1, nc):
        block_send(n).wait_recv()
        total = total + mrecv[n]
    a[ranks:, :] = total * unit
    for at in range(0, ranks, TOP):
        low, high = at + TOP, a.shape[0]
        if low < ranks:
            update(low, low + TOP, at, inverse)
            later = inverted(low // TOP)
            update(low + TOP, high, at, inverse)
            inverse = later
        else:
            update(low, high, at, inverse)
    solved = a[ranks:, :]
    parts[me_r, me_c] = jnp.sum(solved * solved, axis=0, keepdims=True)

    def part_send(i, k):
        slot = parts.at[me_r, me_c]
        device = {"row": lax.rem(me_r + i, nr), "col": lax.rem(me_c + k, nc)}
        return push(slot, slot, qs.at[i, k], qr.at[i, k], device)

    others = [(i, k) for i in range(nr) for k in range(nc) if i or k]
    for i, k in others:
        part_send(i, k).start()
    solved_ref[...] = solved
    for i, k in others:
        came = parts.at[lax.rem(me_r + nr - i, nr), lax.rem(me_c + nc - k, nc)]
        device = {"row": lax.rem(me_r + i, nr), "col": lax.rem(me_c + k, nc)}
        push(parts.at[me_r, me_c], came, qs.at[i, k], qr.at[i, k], device).wait_recv()
    total = jnp.sum(parts[...].reshape(nr * nc, 1, ranks), axis=0)
    squares_ref[...] = total
    for copy in copies + gcopies + ccopies + rcopies:
        copy.wait_send()
    for n in range(1, nc):
        block_send(n).wait_send()
    for i, k in others:
        part_send(i, k).wait_send()


def local(tensor, factor_b, factor_c):
    depth, rows_i, cols_j = tensor.shape
    ranks = factor_c.shape[1]
    nr, nc = lax.axis_size("row"), lax.axis_size("col")
    share = rows_i // nc
    rows = ranks // (nr * nc)
    f32, bf16 = jnp.float32, jnp.bfloat16
    vmem = pl.BlockSpec(memory_space=pltpu.VMEM)
    hbm = pl.BlockSpec(memory_space=pltpu.HBM)
    dma = pltpu.SemaphoreType.DMA
    solved, squares = pl.pallas_call(
        functools.partial(whole_kernel, nr, nc),
        out_shape=(jax.ShapeDtypeStruct((share, ranks), f32), jax.ShapeDtypeStruct((1, ranks), f32)),
        in_specs=[hbm, hbm, hbm],
        out_specs=(vmem, vmem),
        scratch_shapes=[
            pltpu.VMEM((ranks, cols_j), f32),
            pltpu.VMEM((3 * cols_j, ranks), bf16),
            pltpu.VMEM((ranks, ranks), f32),
            pltpu.VMEM((nc, rows, ranks), f32),
            pltpu.VMEM((nc, rows, ranks), f32),
            pltpu.VMEM((nr, nc, rows, ranks), f32),
            pltpu.VMEM((nc, share, ranks), f32),
            pltpu.VMEM((nc, share, ranks), f32),
            pltpu.VMEM((nc, depth, share, cols_j), f32),
            pltpu.VMEM((nc, depth * share, 2 * cols_j), bf16),
            pltpu.VMEM((depth, ranks), f32),
            pltpu.VMEM((ranks + share, ranks), f32),
            pltpu.VMEM((nr, nc, 1, ranks), f32),
            dma((nc,)), dma((2,)), dma((nr,)), dma((nr,)), dma((nc,)), dma((nc,)), dma((nc,)), dma((nc,)),
            dma((nr,)), dma((nr,)), dma((nc,)), dma((nc,)), dma((nr, nc)), dma((nr, nc)),
        ],
        compiler_params=pltpu.CompilerParams(
            collective_id=0, has_side_effects=True, vmem_limit_bytes=62 * 2**20
        ),
        name="whole",
    )(tensor, factor_b.T, factor_c)
    col_scale = jnp.sqrt(squares / (rows_i * nr) + eps)
    return (solved / col_scale, col_scale.reshape(ranks))


def solution(mesh):
    return jax.shard_map(
        local,
        mesh=mesh,
        in_specs=(P(None, "row", "col"), P("col", "row"), P()),
        out_specs=(P(("row", "col"), None), P()),
        check_vma=False,
    )
```

```python
import functools

import jax
import jax.numpy as jnp
from jax import lax
from jax.experimental import pallas as pl
from jax.experimental.pallas import tpu as pltpu
from jax.sharding import PartitionSpec as P

eps = 1e-06
MESH = pl.DeviceIdType.MESH
HIGH = lax.Precision.HIGHEST
TOP = 64
SUB = 8


def push(src, dst, ssem, rsem, device):
    return pltpu.make_async_remote_copy(
        src_ref=src, dst_ref=dst, send_sem=ssem, recv_sem=rsem,
        device_id=device, device_id_type=MESH,
    )


def greet(nr, nc):
    me_r, me_c = lax.axis_index("row"), lax.axis_index("col")
    barrier = pltpu.get_barrier_semaphore()
    for n in range(1, nr):
        pl.semaphore_signal(barrier, inc=1, device_id={"row": lax.rem(me_r + n, nr)}, device_id_type=MESH)
    for n in range(1, nc):
        pl.semaphore_signal(barrier, inc=1, device_id={"col": lax.rem(me_c + n, nc)}, device_id_type=MESH)
    return lambda: pl.semaphore_wait(barrier, nr + nc - 2)


def nt_dot(a, b, precision=None):
    return lax.dot_general(
        a, b, (((1,), (1,)), ((), ())), precision=precision, preferred_element_type=jnp.float32
    )


def line(held, p):
    return jnp.broadcast_to(held[p:p + 1], held.shape)


def invert_block(tile, low):
    size = TOP // SUB
    lane = lax.broadcasted_iota(jnp.int32, (SUB, 2 * TOP), 1)
    row = lax.broadcasted_iota(jnp.int32, (SUB, 2 * TOP), 0)
    held = (lane < TOP) if low else (lane >= TOP)
    shift = TOP if low else 0
    base = 0 if low else TOP
    v = []
    for i in range(size):
        unit = (lane == row + (shift + i * SUB)).astype(jnp.float32)
        v.append(jnp.where(held, tile[i * SUB:(i + 1) * SUB], unit))
    wide = (SUB, 2 * TOP)
    for s in range(size):
        cols = [
            [jnp.broadcast_to(v[i][:, base + s * SUB + j:base + s * SUB + j + 1], wide) for j in range(SUB)]
            for i in range(size)
        ]
        head, c = v[s], list(cols[s])
        for p in range(0, SUB, 2):
            cp, cq = c[p], c[p + 1]
            first, second = row == p, row == p + 1
            here = first | second
            a, d = line(cp, p), line(cq, p + 1)
            b, e = line(cq, p), line(cp, p + 1)
            inv = pl.reciprocal(a * d - b * e, approx=True)
            cp = jnp.where(first, -1.0, jnp.where(second, 0.0, cp))
            cq = jnp.where(second, -1.0, jnp.where(first, 0.0, cq))

            def step(held):
                x, y = line(held, p), line(held, p + 1)
                change = cp * (d * x - b * y) + cq * (a * y - e * x)
                return jnp.where(here, 0.0, held) - change * inv

            for j in range(p + 2, SUB):
                c[j] = step(c[j])
            head = step(head)
        lines = [line(head, j) for j in range(SUB)]
        for i in range(size):
            if i == s:
                v[i] = head
            else:
                terms = [cols[i][j] * lines[j] for j in range(SUB)]
                while len(terms) > 1:
                    terms = [a + b for a, b in zip(terms[::2], terms[1::2])]
                v[i] = v[i] - terms[0]
    whole = jnp.concatenate(v, axis=0)
    return whole[:, shift:shift + TOP]


def whole_kernel(
    nr, nc, t_ref, b_hbm, c_hbm, solved_ref, squares_ref,
    bt, bcat, gc, gsend, grecv, gfull, msend, mrecv, tbuf, tcat, c_ref, a, parts,
    tsem, lsem, bs, br, gs, gr_, cs, cr, rs, rr, ms, mr, qs, qr,
):
    me_r, me_c = lax.axis_index("row"), lax.axis_index("col")
    depth, share = tbuf.shape[1], tbuf.shape[2]
    rb = b_hbm.shape[0]
    rows = gsend.shape[1]
    ranks = bt.shape[0]

    def load(n):
        p = lax.rem(me_c + n, nc)
        start = pl.multiple_of(p * share, share)
        return pltpu.make_async_copy(t_ref.at[:, pl.ds(start, share), :], tbuf.at[n], tsem.at[n])

    greeted = greet(nr, nc)
    mine_rows = pl.ds(pl.multiple_of(me_r * rb, rb), rb)
    own_copy = pltpu.make_async_copy(b_hbm, bt.at[mine_rows], lsem.at[0])
    c_copy = pltpu.make_async_copy(c_hbm, c_ref, lsem.at[1])
    own_copy.start()
    c_copy.start()
    early = nc // 4
    for n in range(1, early + 1):
        load(n).start()
    greeted()

    mate = me_r + 1 - 2 * lax.rem(me_r, 2)
    hops = range(2, nr, 2)

    def slab(n):
        return lax.rem(me_r + nr - n, nr)

    def passed(n):
        return lax.rem(mate + nr - n, nr)

    def row_copy(src, dst, ssems, rsems, n, r):
        return push(src, dst, ssems.at[n], rsems.at[n], {"row": r})

    def place(r):
        return bt.at[pl.ds(pl.multiple_of(r * rb, rb), rb)]

    def gram_place(r):
        return gfull.at[r]

    def spread(src, at, ssems, rsems):
        made = [row_copy(src, at(me_r), ssems, rsems, n, lax.rem(me_r + n, nr)) for n in hops]
        made.append(row_copy(src, at(me_r), ssems, rsems, 1, mate))
        for copy in made:
            copy.start()
        return made

    def hand_on(at, ssems, rsems):
        made = []
        for n in hops:
            row_copy(at(slab(n)), at(slab(n)), ssems, rsems, n, lax.rem(me_r + n, nr)).wait_recv()
            made.append(row_copy(at(slab(n)), at(slab(n)), ssems, rsems, n + 1, mate))
            made[-1].start()
        return made

    def gathered(at, ssems, rsems):
        row_copy(at(mate), at(mate), ssems, rsems, 1, mate).wait_recv()
        for n in hops:
            row_copy(at(passed(n)), at(passed(n)), ssems, rsems, n + 1, mate).wait_recv()

    copies = spread(b_hbm, place, bs, br)
    for n in list(range(early + 1, nc)) + [0]:
        load(n).start()
    c_copy.wait()
    c = c_ref[...]
    gc[...] = lax.dot_general(
        c, c, (((0,), (0,)), ((), ())), precision=HIGH, preferred_element_type=jnp.float32
    )
    group = max(1, 512 // share)
    wide = tbuf.shape[3]

    def split(step):
        n = lax.rem(step, nc)
        load(n).wait()
        for g in range(0, depth, group):
            slab = tbuf[n, g:g + group].reshape(group * share, wide)
            th = slab.astype(jnp.bfloat16)
            tcat[n, g * share:(g + group) * share, :wide] = th
            tcat[n, g * share:(g + group) * share, wide:] = (slab - th.astype(jnp.float32)).astype(jnp.bfloat16)

    pl.loop(1, nc // 2 + 1)(split)
    copies += hand_on(place, bs, br)
    pl.loop(nc // 2 + 1, nc + 1)(split)
    gathered(place, bs, br)

    own_copy.wait()
    full = bt[...]
    own = bt[mine_rows, :]
    part = nt_dot(own, full, HIGH)
    for n in range(nc):
        gsend[n] = part[n * rows:(n + 1) * rows]
    gcopies = []
    for n in range(1, nc):
        p = lax.rem(me_c + n, nc)
        gcopies.append(push(gsend.at[p], grecv.at[n], gs.at[n], gr_.at[n], {"col": p}))
        gcopies[-1].start()
    turned = full.T
    hi = turned.astype(jnp.bfloat16)
    lo = (turned - hi.astype(jnp.float32)).astype(jnp.bfloat16)
    bcat[...] = jnp.concatenate([hi, hi, lo], axis=0)

    def block(n):
        total = jnp.zeros((share, ranks), jnp.float32)
        for g in range(0, depth, group):
            halves = tcat[n, g * share:(g + group) * share, :]
            product = jnp.dot(
                jnp.concatenate([halves, halves[:, :wide]], axis=1), bcat[...], preferred_element_type=jnp.float32
            )
            for f in range(group):
                total += product[f * share:(f + 1) * share] * c_ref[g + f:g + f + 1, :]
        msend[n] = total

    def block_send(n):
        return push(msend.at[n], mrecv.at[n], ms.at[n], mr.at[n], {"col": lax.rem(me_c + n, nc)})

    def blocks(first, last):
        @pl.loop(first, last)
        def _(n):
            block(n)
            block_send(n).start()

    cuts = [1 + nc * k // 4 for k in range(4)] + [nc]
    blocks(cuts[0], cuts[1])
    for copy in gcopies:
        copy.wait_recv()
    total = gsend[me_c]
    for n in range(1, nc):
        total = total + grecv[n]
    gfull[me_r, me_c] = total
    for n in range(1, nc):
        slot = gfull.at[me_r, me_c]
        copies.append(push(slot, slot, cs.at[n], cr.at[n], {"col": lax.rem(me_c + n, nc)}))
        copies[-1].start()
    blocks(cuts[1], cuts[2])
    for n in range(1, nc):
        came = gfull.at[me_r, lax.rem(me_c + nc - n, nc)]
        push(gfull.at[me_r, me_c], came, cs.at[n], cr.at[n], {"col": lax.rem(me_c + n, nc)}).wait_recv()
    copies += spread(gfull.at[me_r], gram_place, rs, rr)
    blocks(cuts[2], cuts[3])
    copies += hand_on(gram_place, rs, rr)
    blocks(cuts[3], cuts[4])
    block(0)
    gathered(gram_place, rs, rr)
    lanes = lax.broadcasted_iota(jnp.int32, (rows, ranks), 1)
    subs = lax.broadcasted_iota(jnp.int32, (rows, ranks), 0)
    diagonal = jnp.zeros((rows, ranks), jnp.float32)
    for r in range(nr):
        for k in range(nc):
            at = (r * nc + k) * rows
            held = gfull[r, k] * gc[at:at + rows, :]
            a[at:at + rows, :] = held
            diagonal = jnp.where(lanes == subs + at, held, diagonal)
    unit = 1.0 / jnp.sum(diagonal, axis=0, keepdims=True)
    a[0:ranks, :] = a[0:ranks, :] * unit

    def inverted(b):
        at = b * TOP
        return invert_block(a[at:at + TOP, (b // 2) * 2 * TOP:(b // 2 + 1) * 2 * TOP], b % 2 == 0)

    def update(low, high, at, inverse):
        held = a[low:high, :]
        w = jnp.dot(held[:, at:at + TOP], inverse, precision=HIGH, preferred_element_type=jnp.float32)
        change = jnp.dot(w, a[at:at + TOP, :], precision=HIGH, preferred_element_type=jnp.float32)
        a[low:high, :] = held - change
        a[low:high, at:at + TOP] = w

    inverse = inverted(0)
    total = msend[0]
    for n in range(1, nc):
        block_send(n).wait_recv()
        total = total + mrecv[n]
    a[ranks:, :] = total * unit
    for at in range(0, ranks, TOP):
        low, high = at + TOP, a.shape[0]
        if low < ranks:
            update(low, low + TOP, at, inverse)
            later = inverted(low // TOP)
            update(low + TOP, high, at, inverse)
            inverse = later
        else:
            update(low, high, at, inverse)
    solved = a[ranks:, :]
    parts[me_r, me_c] = jnp.sum(solved * solved, axis=0, keepdims=True)

    def part_send(i, k):
        slot = parts.at[me_r, me_c]
        device = {"row": lax.rem(me_r + i, nr), "col": lax.rem(me_c + k, nc)}
        return push(slot, slot, qs.at[i, k], qr.at[i, k], device)

    others = [(i, k) for i in range(nr) for k in range(nc) if i or k]
    for i, k in others:
        part_send(i, k).start()
    solved_ref[...] = solved
    for i, k in others:
        came = parts.at[lax.rem(me_r + nr - i, nr), lax.rem(me_c + nc - k, nc)]
        device = {"row": lax.rem(me_r + i, nr), "col": lax.rem(me_c + k, nc)}
        push(parts.at[me_r, me_c], came, qs.at[i, k], qr.at[i, k], device).wait_recv()
    total = jnp.sum(parts[...].reshape(nr * nc, 1, ranks), axis=0)
    squares_ref[...] = total
    for copy in copies + gcopies:
        copy.wait_send()
    for n in range(1, nc):
        block_send(n).wait_send()
    for i, k in others:
        part_send(i, k).wait_send()


def local(tensor, factor_b, factor_c):
    depth, rows_i, cols_j = tensor.shape
    ranks = factor_c.shape[1]
    nr, nc = lax.axis_size("row"), lax.axis_size("col")
    share = rows_i // nc
    rows = ranks // (nr * nc)
    f32, bf16 = jnp.float32, jnp.bfloat16
    vmem = pl.BlockSpec(memory_space=pltpu.VMEM)
    hbm = pl.BlockSpec(memory_space=pltpu.HBM)
    dma = pltpu.SemaphoreType.DMA
    solved, squares = pl.pallas_call(
        functools.partial(whole_kernel, nr, nc),
        out_shape=(jax.ShapeDtypeStruct((share, ranks), f32), jax.ShapeDtypeStruct((1, ranks), f32)),
        in_specs=[hbm, hbm, hbm],
        out_specs=(vmem, vmem),
        scratch_shapes=[
            pltpu.VMEM((ranks, cols_j), f32),
            pltpu.VMEM((3 * cols_j, ranks), bf16),
            pltpu.VMEM((ranks, ranks), f32),
            pltpu.VMEM((nc, rows, ranks), f32),
            pltpu.VMEM((nc, rows, ranks), f32),
            pltpu.VMEM((nr, nc, rows, ranks), f32),
            pltpu.VMEM((nc, share, ranks), f32),
            pltpu.VMEM((nc, share, ranks), f32),
            pltpu.VMEM((nc, depth, share, cols_j), f32),
            pltpu.VMEM((nc, depth * share, 2 * cols_j), bf16),
            pltpu.VMEM((depth, ranks), f32),
            pltpu.VMEM((ranks + share, ranks), f32),
            pltpu.VMEM((nr, nc, 1, ranks), f32),
            dma((nc,)), dma((2,)), dma((nr,)), dma((nr,)), dma((nc,)), dma((nc,)), dma((nc,)), dma((nc,)),
            dma((nr,)), dma((nr,)), dma((nc,)), dma((nc,)), dma((nr, nc)), dma((nr, nc)),
        ],
        compiler_params=pltpu.CompilerParams(
            collective_id=0, has_side_effects=True, vmem_limit_bytes=56 * 2**20
        ),
        name="whole",
    )(tensor, factor_b.T, factor_c)
    col_scale = jnp.sqrt(squares / (rows_i * nr) + eps)
    return (solved / col_scale, col_scale.reshape(ranks))


def solution(mesh):
    return jax.shard_map(
        local,
        mesh=mesh,
        in_specs=(P(None, "row", "col"), P("col", "row"), P()),
        out_specs=(P(("row", "col"), None), P()),
        check_vma=False,
    )
```

```python
import functools

import jax
import jax.numpy as jnp
from jax import lax
from jax.experimental import pallas as pl
from jax.experimental.pallas import tpu as pltpu
from jax.sharding import PartitionSpec as P

eps = 1e-06
MESH = pl.DeviceIdType.MESH
HIGH = lax.Precision.HIGHEST
TOP = 64
SUB = 8


def push(src, dst, ssem, rsem, device):
    return pltpu.make_async_remote_copy(
        src_ref=src, dst_ref=dst, send_sem=ssem, recv_sem=rsem,
        device_id=device, device_id_type=MESH,
    )


def greet(nr, nc):
    me_r, me_c = lax.axis_index("row"), lax.axis_index("col")
    barrier = pltpu.get_barrier_semaphore()
    for n in range(1, nr):
        pl.semaphore_signal(barrier, inc=1, device_id={"row": lax.rem(me_r + n, nr)}, device_id_type=MESH)
    for n in range(1, nc):
        pl.semaphore_signal(barrier, inc=1, device_id={"col": lax.rem(me_c + n, nc)}, device_id_type=MESH)
    return lambda: pl.semaphore_wait(barrier, nr + nc - 2)


def nt_dot(a, b, precision=None):
    return lax.dot_general(
        a, b, (((1,), (1,)), ((), ())), precision=precision, preferred_element_type=jnp.float32
    )


def line(held, p):
    return jnp.broadcast_to(held[p:p + 1], held.shape)


def invert_block(tile, low):
    size = TOP // SUB
    lane = lax.broadcasted_iota(jnp.int32, (SUB, 2 * TOP), 1)
    row = lax.broadcasted_iota(jnp.int32, (SUB, 2 * TOP), 0)
    held = (lane < TOP) if low else (lane >= TOP)
    shift = TOP if low else 0
    base = 0 if low else TOP
    v = []
    for i in range(size):
        unit = (lane == row + (shift + i * SUB)).astype(jnp.float32)
        v.append(jnp.where(held, tile[i * SUB:(i + 1) * SUB], unit))
    wide = (SUB, 2 * TOP)
    for s in range(size):
        cols = [
            [jnp.broadcast_to(v[i][:, base + s * SUB + j:base + s * SUB + j + 1], wide) for j in range(SUB)]
            for i in range(size)
        ]
        head, c = v[s], list(cols[s])
        for p in range(0, SUB, 2):
            cp, cq = c[p], c[p + 1]
            first, second = row == p, row == p + 1
            here = first | second
            a, d = line(cp, p), line(cq, p + 1)
            b, e = line(cq, p), line(cp, p + 1)
            inv = pl.reciprocal(a * d - b * e, approx=True)
            cp = jnp.where(first, -1.0, jnp.where(second, 0.0, cp))
            cq = jnp.where(second, -1.0, jnp.where(first, 0.0, cq))

            def step(held):
                x, y = line(held, p), line(held, p + 1)
                change = cp * (d * x - b * y) + cq * (a * y - e * x)
                return jnp.where(here, 0.0, held) - change * inv

            for j in range(p + 2, SUB):
                c[j] = step(c[j])
            head = step(head)
        lines = [line(head, j) for j in range(SUB)]
        for i in range(size):
            if i == s:
                v[i] = head
            else:
                terms = [cols[i][j] * lines[j] for j in range(SUB)]
                while len(terms) > 1:
                    terms = [a + b for a, b in zip(terms[::2], terms[1::2])]
                v[i] = v[i] - terms[0]
    whole = jnp.concatenate(v, axis=0)
    return whole[:, shift:shift + TOP]


def whole_kernel(
    nr, nc, t_ref, b_hbm, c_hbm, solved_ref, squares_ref,
    bt, bcat, gc, gsend, grecv, gfull, msend, mrecv, tbuf, tcat, c_ref, a, parts,
    tsem, lsem, bs, br, gs, gr_, cs, cr, rs, rr, ms, mr, qs, qr,
):
    me_r, me_c = lax.axis_index("row"), lax.axis_index("col")
    depth, share = tbuf.shape[1], tbuf.shape[2]
    rb = b_hbm.shape[0]
    rows = gsend.shape[1]
    ranks = bt.shape[0]

    def load(n):
        p = lax.rem(me_c + n, nc)
        start = pl.multiple_of(p * share, share)
        return pltpu.make_async_copy(t_ref.at[:, pl.ds(start, share), :], tbuf.at[n], tsem.at[n])

    greeted = greet(nr, nc)
    mine_rows = pl.ds(pl.multiple_of(me_r * rb, rb), rb)
    own_copy = pltpu.make_async_copy(b_hbm, bt.at[mine_rows], lsem.at[0])
    c_copy = pltpu.make_async_copy(c_hbm, c_ref, lsem.at[1])
    own_copy.start()
    c_copy.start()
    for n in list(range(1, nc)) + [0]:
        load(n).start()
    greeted()

    copies = []
    for n in range(1, nr):
        copies.append(push(b_hbm, bt.at[mine_rows], bs.at[n], br.at[n], {"row": lax.rem(me_r + n, nr)}))
        copies[-1].start()
    c_copy.wait()
    c = c_ref[...]
    gc[...] = lax.dot_general(
        c, c, (((0,), (0,)), ((), ())), precision=HIGH, preferred_element_type=jnp.float32
    )
    group = max(1, 512 // share)
    wide = tbuf.shape[3]

    @pl.loop(1, nc + 1)
    def _(step):
        n = lax.rem(step, nc)
        load(n).wait()
        for g in range(0, depth, group):
            slab = tbuf[n, g:g + group].reshape(group * share, wide)
            th = slab.astype(jnp.bfloat16)
            tcat[step - 1, g * share:(g + group) * share, :wide] = th
            tcat[step - 1, g * share:(g + group) * share, wide:] = (slab - th.astype(jnp.float32)).astype(jnp.bfloat16)

    for n in range(1, nr):
        came = pl.ds(pl.multiple_of(lax.rem(me_r + nr - n, nr) * rb, rb), rb)
        push(b_hbm, bt.at[came], bs.at[n], br.at[n], {"row": lax.rem(me_r + n, nr)}).wait_recv()

    own_copy.wait()
    full = bt[...]
    own = bt[mine_rows, :]
    part = nt_dot(own, full, HIGH)
    for n in range(nc):
        gsend[n] = part[n * rows:(n + 1) * rows]
    gcopies = []
    for n in range(1, nc):
        p = lax.rem(me_c + n, nc)
        gcopies.append(push(gsend.at[p], grecv.at[n], gs.at[n], gr_.at[n], {"col": p}))
        gcopies[-1].start()
    turned = full.T
    hi = turned.astype(jnp.bfloat16)
    lo = (turned - hi.astype(jnp.float32)).astype(jnp.bfloat16)
    bcat[...] = jnp.concatenate([hi, hi, lo], axis=0)

    def pair(q):
        halves = tcat[pl.ds(2 * q, 2)].reshape(2 * depth * share, 2 * wide)
        product = jnp.dot(
            jnp.concatenate([halves, halves[:, :wide]], axis=1), bcat[...], preferred_element_type=jnp.float32
        )
        for u in range(2):
            total = jnp.zeros((share, ranks), jnp.float32)
            for f in range(depth):
                at = (u * depth + f) * share
                total += product[at:at + share] * c_ref[f:f + 1, :]
            msend[lax.rem(2 * q + u + 1, nc)] = total

    def block_send(n):
        return push(msend.at[n], mrecv.at[n], ms.at[n], mr.at[n], {"col": lax.rem(me_c + n, nc)})

    def pairs(first, last):
        @pl.loop(first, last)
        def _(q):
            pair(q)
            block_send(2 * q + 1).start()

            @pl.when(2 * q + 2 < nc)
            def _():
                block_send(2 * q + 2).start()

    cut1, cut2 = nc // 8, nc // 4
    pairs(0, cut1)
    for copy in gcopies:
        copy.wait_recv()
    total = gsend[me_c]
    for n in range(1, nc):
        total = total + grecv[n]
    gfull[me_r, me_c] = total
    ccopies = []
    for n in range(1, nc):
        slot = gfull.at[me_r, me_c]
        ccopies.append(push(slot, slot, cs.at[n], cr.at[n], {"col": lax.rem(me_c + n, nc)}))
        ccopies[-1].start()
    pairs(cut1, cut2)
    for n in range(1, nc):
        came = gfull.at[me_r, lax.rem(me_c + nc - n, nc)]
        push(gfull.at[me_r, me_c], came, cs.at[n], cr.at[n], {"col": lax.rem(me_c + n, nc)}).wait_recv()
    rcopies = []
    for n in range(1, nr):
        slot = gfull.at[me_r]
        rcopies.append(push(slot, slot, rs.at[n], rr.at[n], {"row": lax.rem(me_r + n, nr)}))
        rcopies[-1].start()
    pairs(cut2, nc // 2)
    for n in range(1, nr):
        came = gfull.at[lax.rem(me_r + nr - n, nr)]
        push(gfull.at[me_r], came, rs.at[n], rr.at[n], {"row": lax.rem(me_r + n, nr)}).wait_recv()
    lanes = lax.broadcasted_iota(jnp.int32, (rows, ranks), 1)
    subs = lax.broadcasted_iota(jnp.int32, (rows, ranks), 0)
    diagonal = jnp.zeros((rows, ranks), jnp.float32)
    for r in range(nr):
        for k in range(nc):
            at = (r * nc + k) * rows
            held = gfull[r, k] * gc[at:at + rows, :]
            a[at:at + rows, :] = held
            diagonal = jnp.where(lanes == subs + at, held, diagonal)
    unit = 1.0 / jnp.sum(diagonal, axis=0, keepdims=True)
    a[0:ranks, :] = a[0:ranks, :] * unit

    def inverted(b):
        at = b * TOP
        return invert_block(a[at:at + TOP, (b // 2) * 2 * TOP:(b // 2 + 1) * 2 * TOP], b % 2 == 0)

    def update(low, high, at, inverse):
        held = a[low:high, :]
        w = jnp.dot(held[:, at:at + TOP], inverse, precision=HIGH, preferred_element_type=jnp.float32)
        change = jnp.dot(w, a[at:at + TOP, :], precision=HIGH, preferred_element_type=jnp.float32)
        a[low:high, :] = held - change
        a[low:high, at:at + TOP] = w

    inverse = inverted(0)
    total = msend[0]
    for n in range(1, nc):
        block_send(n).wait_recv()
        total = total + mrecv[n]
    a[ranks:, :] = total * unit
    for at in range(0, ranks, TOP):
        low, high = at + TOP, a.shape[0]
        if low < ranks:
            update(low, low + TOP, at, inverse)
            later = inverted(low // TOP)
            update(low + TOP, high, at, inverse)
            inverse = later
        else:
            update(low, high, at, inverse)
    solved = a[ranks:, :]
    parts[me_r, me_c] = jnp.sum(solved * solved, axis=0, keepdims=True)

    def part_send(i, k):
        slot = parts.at[me_r, me_c]
        device = {"row": lax.rem(me_r + i, nr), "col": lax.rem(me_c + k, nc)}
        return push(slot, slot, qs.at[i, k], qr.at[i, k], device)

    others = [(i, k) for i in range(nr) for k in range(nc) if i or k]
    for i, k in others:
        part_send(i, k).start()
    solved_ref[...] = solved
    for i, k in others:
        came = parts.at[lax.rem(me_r + nr - i, nr), lax.rem(me_c + nc - k, nc)]
        device = {"row": lax.rem(me_r + i, nr), "col": lax.rem(me_c + k, nc)}
        push(parts.at[me_r, me_c], came, qs.at[i, k], qr.at[i, k], device).wait_recv()
    total = jnp.sum(parts[...].reshape(nr * nc, 1, ranks), axis=0)
    squares_ref[...] = total
    for copy in copies + gcopies + ccopies + rcopies:
        copy.wait_send()
    for n in range(1, nc):
        block_send(n).wait_send()
    for i, k in others:
        part_send(i, k).wait_send()


def local(tensor, factor_b, factor_c):
    depth, rows_i, cols_j = tensor.shape
    ranks = factor_c.shape[1]
    nr, nc = lax.axis_size("row"), lax.axis_size("col")
    share = rows_i // nc
    rows = ranks // (nr * nc)
    f32, bf16 = jnp.float32, jnp.bfloat16
    vmem = pl.BlockSpec(memory_space=pltpu.VMEM)
    hbm = pl.BlockSpec(memory_space=pltpu.HBM)
    dma = pltpu.SemaphoreType.DMA
    solved, squares = pl.pallas_call(
        functools.partial(whole_kernel, nr, nc),
        out_shape=(jax.ShapeDtypeStruct((share, ranks), f32), jax.ShapeDtypeStruct((1, ranks), f32)),
        in_specs=[hbm, hbm, hbm],
        out_specs=(vmem, vmem),
        scratch_shapes=[
            pltpu.VMEM((ranks, cols_j), f32),
            pltpu.VMEM((3 * cols_j, ranks), bf16),
            pltpu.VMEM((ranks, ranks), f32),
            pltpu.VMEM((nc, rows, ranks), f32),
            pltpu.VMEM((nc, rows, ranks), f32),
            pltpu.VMEM((nr, nc, rows, ranks), f32),
            pltpu.VMEM((nc, share, ranks), f32),
            pltpu.VMEM((nc, share, ranks), f32),
            pltpu.VMEM((nc, depth, share, cols_j), f32),
            pltpu.VMEM((nc, depth * share, 2 * cols_j), bf16),
            pltpu.VMEM((depth, ranks), f32),
            pltpu.VMEM((ranks + share, ranks), f32),
            pltpu.VMEM((nr, nc, 1, ranks), f32),
            dma((nc,)), dma((2,)), dma((nr,)), dma((nr,)), dma((nc,)), dma((nc,)), dma((nc,)), dma((nc,)),
            dma((nr,)), dma((nr,)), dma((nc,)), dma((nc,)), dma((nr, nc)), dma((nr, nc)),
        ],
        compiler_params=pltpu.CompilerParams(
            collective_id=0, has_side_effects=True, vmem_limit_bytes=62 * 2**20
        ),
        name="whole",
    )(tensor, factor_b.T, factor_c)
    col_scale = jnp.sqrt(squares / (rows_i * nr) + eps)
    return (solved / col_scale, col_scale.reshape(ranks))


def solution(mesh):
    return jax.shard_map(
        local,
        mesh=mesh,
        in_specs=(P(None, "row", "col"), P("col", "row"), P()),
        out_specs=(P(("row", "col"), None), P()),
        check_vma=False,
    )
```

```python
import functools

import jax
import jax.numpy as jnp
from jax import lax
from jax.experimental import pallas as pl
from jax.experimental.pallas import tpu as pltpu
from jax.sharding import PartitionSpec as P

eps = 1e-06
MESH = pl.DeviceIdType.MESH
HIGH = lax.Precision.HIGHEST
TOP = 64
SUB = 8


def push(src, dst, ssem, rsem, device):
    return pltpu.make_async_remote_copy(
        src_ref=src, dst_ref=dst, send_sem=ssem, recv_sem=rsem,
        device_id=device, device_id_type=MESH,
    )


def greet(nr, nc):
    me_r, me_c = lax.axis_index("row"), lax.axis_index("col")
    barrier = pltpu.get_barrier_semaphore()
    for n in range(1, nr):
        pl.semaphore_signal(barrier, inc=1, device_id={"row": lax.rem(me_r + n, nr)}, device_id_type=MESH)
    for n in range(1, nc):
        pl.semaphore_signal(barrier, inc=1, device_id={"col": lax.rem(me_c + n, nc)}, device_id_type=MESH)
    return lambda: pl.semaphore_wait(barrier, nr + nc - 2)


def nt_dot(a, b, precision=None):
    return lax.dot_general(
        a, b, (((1,), (1,)), ((), ())), precision=precision, preferred_element_type=jnp.float32
    )


def line(held, p):
    return jnp.broadcast_to(held[p:p + 1], held.shape)


def invert_block(tile, low):
    size = TOP // SUB
    lane = lax.broadcasted_iota(jnp.int32, (SUB, 2 * TOP), 1)
    row = lax.broadcasted_iota(jnp.int32, (SUB, 2 * TOP), 0)
    held = (lane < TOP) if low else (lane >= TOP)
    shift = TOP if low else 0
    base = 0 if low else TOP
    v = []
    for i in range(size):
        unit = (lane == row + (shift + i * SUB)).astype(jnp.float32)
        v.append(jnp.where(held, tile[i * SUB:(i + 1) * SUB], unit))
    wide = (SUB, 2 * TOP)
    for s in range(size):
        cols = [
            [jnp.broadcast_to(v[i][:, base + s * SUB + j:base + s * SUB + j + 1], wide) for j in range(SUB)]
            for i in range(size)
        ]
        head, c = v[s], list(cols[s])
        for p in range(0, SUB, 2):
            cp, cq = c[p], c[p + 1]
            first, second = row == p, row == p + 1
            here = first | second
            a, d = line(cp, p), line(cq, p + 1)
            b, e = line(cq, p), line(cp, p + 1)
            inv = pl.reciprocal(a * d - b * e, approx=True)
            cp = jnp.where(first, -1.0, jnp.where(second, 0.0, cp))
            cq = jnp.where(second, -1.0, jnp.where(first, 0.0, cq))

            def step(held):
                x, y = line(held, p), line(held, p + 1)
                change = cp * (d * x - b * y) + cq * (a * y - e * x)
                return jnp.where(here, 0.0, held) - change * inv

            for j in range(p + 2, SUB):
                c[j] = step(c[j])
            head = step(head)
        lines = [line(head, j) for j in range(SUB)]
        for i in range(size):
            if i == s:
                v[i] = head
            else:
                terms = [cols[i][j] * lines[j] for j in range(SUB)]
                while len(terms) > 1:
                    terms = [a + b for a, b in zip(terms[::2], terms[1::2])]
                v[i] = v[i] - terms[0]
    whole = jnp.concatenate(v, axis=0)
    return whole[:, shift:shift + TOP]


def whole_kernel(
    nr, nc, t_ref, b_hbm, c_hbm, solved_ref, squares_ref,
    bt, bcat, gc, gsend, grecv, gfull, msend, mrecv, tbuf, tcat, c_ref, a, parts,
    tsem, lsem, bs, br, gs, gr_, cs, cr, rs, rr, ms, mr, qs, qr,
):
    me_r, me_c = lax.axis_index("row"), lax.axis_index("col")
    depth, share = tbuf.shape[1], tbuf.shape[2]
    rb = b_hbm.shape[0]
    rows = gsend.shape[1]
    ranks = bt.shape[0]

    def load(n):
        p = lax.rem(me_c + n, nc)
        start = pl.multiple_of(p * share, share)
        return pltpu.make_async_copy(t_ref.at[:, pl.ds(start, share), :], tbuf.at[n], tsem.at[n])

    greeted = greet(nr, nc)
    mine_rows = pl.ds(pl.multiple_of(me_r * rb, rb), rb)
    own_copy = pltpu.make_async_copy(b_hbm, bt.at[mine_rows], lsem.at[0])
    c_copy = pltpu.make_async_copy(c_hbm, c_ref, lsem.at[1])
    own_copy.start()
    c_copy.start()
    for n in list(range(1, nc)) + [0]:
        load(n).start()
    greeted()

    copies = []
    for n in range(1, nr):
        copies.append(push(b_hbm, bt.at[mine_rows], bs.at[n], br.at[n], {"row": lax.rem(me_r + n, nr)}))
        copies[-1].start()
    c_copy.wait()
    c = c_ref[...]
    gc[...] = lax.dot_general(
        c, c, (((0,), (0,)), ((), ())), precision=HIGH, preferred_element_type=jnp.float32
    )
    group = max(1, 512 // share)
    wide = tbuf.shape[3]

    @pl.loop(1, nc + 1)
    def _(step):
        n = lax.rem(step, nc)
        load(n).wait()
        for g in range(0, depth, group):
            slab = tbuf[n, g:g + group].reshape(group * share, wide)
            th = slab.astype(jnp.bfloat16)
            tcat[step - 1, g * share:(g + group) * share, :wide] = th
            tcat[step - 1, g * share:(g + group) * share, 2 * wide:] = th
            tcat[step - 1, g * share:(g + group) * share, wide:2 * wide] = (slab - th.astype(jnp.float32)).astype(jnp.bfloat16)

    for n in range(1, nr):
        came = pl.ds(pl.multiple_of(lax.rem(me_r + nr - n, nr) * rb, rb), rb)
        push(b_hbm, bt.at[came], bs.at[n], br.at[n], {"row": lax.rem(me_r + n, nr)}).wait_recv()

    own_copy.wait()
    full = bt[...]
    own = bt[mine_rows, :]
    part = nt_dot(own, full, HIGH)
    for n in range(nc):
        gsend[n] = part[n * rows:(n + 1) * rows]
    gcopies = []
    for n in range(1, nc):
        p = lax.rem(me_c + n, nc)
        gcopies.append(push(gsend.at[p], grecv.at[n], gs.at[n], gr_.at[n], {"col": p}))
        gcopies[-1].start()
    turned = full.T
    hi = turned.astype(jnp.bfloat16)
    lo = (turned - hi.astype(jnp.float32)).astype(jnp.bfloat16)
    bcat[...] = jnp.concatenate([hi, hi, lo], axis=0)

    def pair(q):
        halves = tcat[pl.ds(2 * q, 2)].reshape(2 * depth * share, 3 * wide)
        product = jnp.dot(halves, bcat[...], preferred_element_type=jnp.float32)
        for u in range(2):
            total = jnp.zeros((share, ranks), jnp.float32)
            for f in range(depth):
                at = (u * depth + f) * share
                total += product[at:at + share] * c_ref[f:f + 1, :]
            msend[lax.rem(2 * q + u + 1, nc)] = total

    def block_send(n):
        return push(msend.at[n], mrecv.at[n], ms.at[n], mr.at[n], {"col": lax.rem(me_c + n, nc)})

    def pairs(first, last):
        pl.loop(first, last)(pair)

    def send_pairs(first, last):
        for n in range(2 * first + 1, min(2 * last + 1, nc)):
            block_send(n).start()

    cut1, cut2 = nc // 8, nc // 4
    pairs(0, cut1)
    for copy in gcopies:
        copy.wait_recv()
    total = gsend[me_c]
    for n in range(1, nc):
        total = total + grecv[n]
    gfull[me_r, me_c] = total
    ccopies = []
    for n in range(1, nc):
        slot = gfull.at[me_r, me_c]
        ccopies.append(push(slot, slot, cs.at[n], cr.at[n], {"col": lax.rem(me_c + n, nc)}))
        ccopies[-1].start()
    send_pairs(0, cut1)
    pairs(cut1, cut2)
    for n in range(1, nc):
        came = gfull.at[me_r, lax.rem(me_c + nc - n, nc)]
        push(gfull.at[me_r, me_c], came, cs.at[n], cr.at[n], {"col": lax.rem(me_c + n, nc)}).wait_recv()
    rcopies = []
    for n in range(1, nr):
        slot = gfull.at[me_r]
        rcopies.append(push(slot, slot, rs.at[n], rr.at[n], {"row": lax.rem(me_r + n, nr)}))
        rcopies[-1].start()
    send_pairs(cut1, cut2)
    middle = (cut2 + nc // 2) // 2
    pairs(cut2, middle)
    send_pairs(cut2, middle)
    pairs(middle, nc // 2)
    send_pairs(middle, nc // 2)
    for n in range(1, nr):
        came = gfull.at[lax.rem(me_r + nr - n, nr)]
        push(gfull.at[me_r], came, rs.at[n], rr.at[n], {"row": lax.rem(me_r + n, nr)}).wait_recv()
    lanes = lax.broadcasted_iota(jnp.int32, (rows, ranks), 1)
    subs = lax.broadcasted_iota(jnp.int32, (rows, ranks), 0)
    diagonal = jnp.zeros((rows, ranks), jnp.float32)
    for r in range(nr):
        for k in range(nc):
            at = (r * nc + k) * rows
            held = gfull[r, k] * gc[at:at + rows, :]
            a[at:at + rows, :] = held
            diagonal = jnp.where(lanes == subs + at, held, diagonal)
    unit = 1.0 / jnp.sum(diagonal, axis=0, keepdims=True)
    a[0:ranks, :] = a[0:ranks, :] * unit

    def inverted(b):
        at = b * TOP
        return invert_block(a[at:at + TOP, (b // 2) * 2 * TOP:(b // 2 + 1) * 2 * TOP], b % 2 == 0)

    def update(low, high, at, inverse):
        held = a[low:high, :]
        w = jnp.dot(held[:, at:at + TOP], inverse, precision=HIGH, preferred_element_type=jnp.float32)
        change = jnp.dot(w, a[at:at + TOP, :], precision=HIGH, preferred_element_type=jnp.float32)
        a[low:high, :] = held - change
        a[low:high, at:at + TOP] = w

    inverse = inverted(0)
    total = msend[0]
    for n in range(1, nc):
        block_send(n).wait_recv()
        total = total + mrecv[n]
    a[ranks:, :] = total * unit
    for at in range(0, ranks, TOP):
        low, high = at + TOP, a.shape[0]
        if low < ranks:
            update(low, low + TOP, at, inverse)
            later = inverted(low // TOP)
            update(low + TOP, high, at, inverse)
            inverse = later
        else:
            update(low, high, at, inverse)
    solved = a[ranks:, :]
    parts[me_r, me_c] = jnp.sum(solved * solved, axis=0, keepdims=True)

    def part_send(i, k):
        slot = parts.at[me_r, me_c]
        device = {"row": lax.rem(me_r + i, nr), "col": lax.rem(me_c + k, nc)}
        return push(slot, slot, qs.at[i, k], qr.at[i, k], device)

    others = [(i, k) for i in range(nr) for k in range(nc) if i or k]
    for i, k in others:
        part_send(i, k).start()
    solved_ref[...] = solved
    for i, k in others:
        came = parts.at[lax.rem(me_r + nr - i, nr), lax.rem(me_c + nc - k, nc)]
        device = {"row": lax.rem(me_r + i, nr), "col": lax.rem(me_c + k, nc)}
        push(parts.at[me_r, me_c], came, qs.at[i, k], qr.at[i, k], device).wait_recv()
    total = jnp.sum(parts[...].reshape(nr * nc, 1, ranks), axis=0)
    squares_ref[...] = total
    for copy in copies + gcopies + ccopies + rcopies:
        copy.wait_send()
    for n in range(1, nc):
        block_send(n).wait_send()
    for i, k in others:
        part_send(i, k).wait_send()


def local(tensor, factor_b, factor_c):
    depth, rows_i, cols_j = tensor.shape
    ranks = factor_c.shape[1]
    nr, nc = lax.axis_size("row"), lax.axis_size("col")
    share = rows_i // nc
    rows = ranks // (nr * nc)
    f32, bf16 = jnp.float32, jnp.bfloat16
    vmem = pl.BlockSpec(memory_space=pltpu.VMEM)
    hbm = pl.BlockSpec(memory_space=pltpu.HBM)
    dma = pltpu.SemaphoreType.DMA
    solved, squares = pl.pallas_call(
        functools.partial(whole_kernel, nr, nc),
        out_shape=(jax.ShapeDtypeStruct((share, ranks), f32), jax.ShapeDtypeStruct((1, ranks), f32)),
        in_specs=[hbm, hbm, hbm],
        out_specs=(vmem, vmem),
        scratch_shapes=[
            pltpu.VMEM((ranks, cols_j), f32),
            pltpu.VMEM((3 * cols_j, ranks), bf16),
            pltpu.VMEM((ranks, ranks), f32),
            pltpu.VMEM((nc, rows, ranks), f32),
            pltpu.VMEM((nc, rows, ranks), f32),
            pltpu.VMEM((nr, nc, rows, ranks), f32),
            pltpu.VMEM((nc, share, ranks), f32),
            pltpu.VMEM((nc, share, ranks), f32),
            pltpu.VMEM((nc, depth, share, cols_j), f32),
            pltpu.VMEM((nc, depth * share, 3 * cols_j), bf16),
            pltpu.VMEM((depth, ranks), f32),
            pltpu.VMEM((ranks + share, ranks), f32),
            pltpu.VMEM((nr, nc, 1, ranks), f32),
            dma((nc,)), dma((2,)), dma((nr,)), dma((nr,)), dma((nc,)), dma((nc,)), dma((nc,)), dma((nc,)),
            dma((nr,)), dma((nr,)), dma((nc,)), dma((nc,)), dma((nr, nc)), dma((nr, nc)),
        ],
        compiler_params=pltpu.CompilerParams(
            collective_id=0, has_side_effects=True, vmem_limit_bytes=62 * 2**20
        ),
        name="whole",
    )(tensor, factor_b.T, factor_c)
    col_scale = jnp.sqrt(squares / (rows_i * nr) + eps)
    return (solved / col_scale, col_scale.reshape(ranks))


def solution(mesh):
    return jax.shard_map(
        local,
        mesh=mesh,
        in_specs=(P(None, "row", "col"), P("col", "row"), P()),
        out_specs=(P(("row", "col"), None), P()),
        check_vma=False,
    )
```
